32 devices in a mesh: req: 4 (over z), mlp: 8 (over y, x, core).
Axes of the slice: x: 2, y: 2, z: 4, core: 2. Of those that a mesh axis runs over, the one named last changes fastest.
Arguments:
- inputs: bfloat16 [2, 384, 4096], P(None, 'mlp', 'req'), may hold values from -6 to 6
- norm_gains: float32 [3, 4096], P(None, 'req'), may hold values from 0.25 to 1.75
- attn_weight: bfloat16 [4096, 12288], P('req', 'mlp'), may hold values from -0.09375 to 0.09375
- up_weight: bfloat16 [4096, 16384], P('req', 'mlp'), may hold values from -0.09375 to 0.09375
- dense_weight: bfloat16 [4096, 4096], P('mlp', 'req'), may hold values from -0.09375 to 0.09375
- down_weight: bfloat16 [16384, 4096], P('mlp', 'req'), may hold values from -0.046875 to 0.046875
- next_weight: bfloat16 [4096, 12288], P('req', 'mlp'), may hold values from -0.09375 to 0.09375
- cache_keys: bfloat16 [256, 128, 4096], P('req', None, 'mlp'), may hold values from -360 to 360
- cache_values: bfloat16 [256, 128, 4096], P('req', None, 'mlp'), may hold values from -6 to 6
- lengths: int32 [48], replicated, may hold values from 1 to 4096, as said below
- slot_table: int32 [2, 256], P(None, 'req'), may hold values from -1 to 47, as said below
- parents: int32 [1, 384], P(None, 'req'), may hold values from 0 to 7
Outputs:
- layer_out: bfloat16 [2, 384, 4096], P(None, 'mlp', 'req')
- next_qkv: bfloat16 [2, 384, 12288], P(None, 'req', 'mlp')
The draws below stay inside these ranges and needn't reach their ends.
Inputs may be any that keep to these rules, and one draw needn't show every extreme that they name: `lengths`: each request has between 1 and 32 pages of 128 tokens; the longest request has exactly 32 full pages. `slot_table`: every page of every request is held by exactly one slot; an empty slot has request -1 and page 0. All requests together hold 220 pages, and in every draw the slots of some index of req are all in use.
All inputs are finite; a program needn't handle non-finite values.
Results may differ from the reference program's by a relative error of at most 0.04.
Values may be sent and summed in bfloat16 or wider, within the bound.
No kernel may reach another device: no remote copies, remote signals or barrier semaphores. Data moves between devices by JAX's collectives and lax.ppermute only.
A program may use at most 128 MiB of HBM per device.

```python
import math
import jax
import jax.numpy as jnp
from jax import lax

D = 4096
HEADS = 32
HD = 128
FF = 16384
ROT = 32
PAGE = 128
BEAM = 8
STEPS = 2
MAXPAGES = 32
SLOTS_DEV = 64
REQUESTS = 48
BEAMS = 384
SLOTS = 256


def page_layout(key):
    base = jax.random.fold_in(key, 11)
    order_key, offset_key, place_key, device_key = jax.random.split(base, 4)
    shifts = jnp.array([0, 2, 3, 4, 4, 5, 5, 5, 5, 5, 5, 5], jnp.int32)
    pattern = jnp.right_shift(jnp.full((12,), MAXPAGES, jnp.int32), shifts)
    counts = jnp.tile(pattern, REQUESTS // 12)
    counts = counts[jax.random.permutation(order_key, REQUESTS)]
    offsets = jax.random.randint(offset_key, (REQUESTS,), 0, PAGE)
    first_top = jnp.argmax(counts == MAXPAGES)
    offsets = jnp.where(jnp.arange(REQUESTS) == first_top, 0, offsets)
    lengths = counts * PAGE - offsets
    total_pages = REQUESTS // 12 * (MAXPAGES + MAXPAGES // 4 + MAXPAGES // 8 + 2 * (MAXPAGES // 16) + 7 * (MAXPAGES // 32))
    owners = jnp.repeat(jnp.arange(REQUESTS, dtype=jnp.int32), counts, total_repeat_length=total_pages)
    starts = jnp.cumsum(counts) - counts
    pages = jnp.arange(total_pages, dtype=jnp.int32) - starts[owners]
    ranking = jax.random.permutation(place_key, SLOTS)
    chosen_device = jax.random.randint(device_key, (), 0, SLOTS // SLOTS_DEV)
    priority = ranking + jnp.where(jnp.arange(SLOTS) // SLOTS_DEV == chosen_device, 0, SLOTS)
    places = jnp.argsort(priority)[:total_pages]
    slot_owner = jnp.full((SLOTS,), -1, jnp.int32).at[places].set(owners)
    slot_page = jnp.zeros((SLOTS,), jnp.int32).at[places].set(pages)
    return (lengths.astype(jnp.int32), jnp.stack([slot_owner, slot_page]))


def draw_lengths(key, part):
    return page_layout(key)[0]


def draw_slot_table(key, part):
    return page_layout(key)[1]


def draw_cache_keys(key, part):
    noise = jnp.clip(jax.random.normal(key, (SLOTS, PAGE, D), jnp.float32), -6.0, 6.0)
    return noise.astype(jnp.bfloat16)


def set_ends(result, rng, low, high):
    shape = result.shape
    spot = [jax.random.randint(jax.random.fold_in(rng, axis), (), 0, shape[axis]) for axis in range(len(shape))]
    result = result.at[tuple(spot)].set(low)
    longest = shape.index(max(shape))
    spot[longest] = (spot[longest] + 1) % shape[longest]
    return result.at[tuple(spot)].set(high)


def block_levels(key, shape, shards, least, high):
    def one(axis_at, blocks):
        heights = jax.random.uniform(jax.random.fold_in(jax.random.fold_in(key, 6), axis_at), (blocks,), jnp.float32, least / len(shards), high / len(shards))
        return jnp.repeat(jnp.exp(heights), shape[axis_at] // blocks).reshape((-1,) + (1,) * (len(shape) - axis_at - 1))

    level = one(*shards[0])
    for cut in shards[1:]:
        level = level * one(*cut)
    return level


def scatter_about(own_key, dims, deviation, most, pieces=(), held_as=jnp.bfloat16):
    gain = block_levels(own_key, dims, pieces, -0.22, 0.18) if pieces else 1.0
    entries = jax.random.normal(own_key, dims, jnp.float32) * deviation * gain
    return jnp.minimum(jnp.maximum(entries, -most), most).astype(held_as)


def setup_inputs(seed: int = 0) -> dict:
    seeds = jax.random.split(jax.random.key(seed), 13)
    inputs = scatter_about(seeds[0], (STEPS, BEAMS, D), 1.0, 6.0, ((1, 8), (2, 4)))
    norm_gains = jnp.clip(1.0 + 0.15 * jax.random.normal(seeds[1], (3, D), jnp.float32), 0.25, 1.75)
    attn_weight = scatter_about(seeds[2], (D, 3 * D), D ** -0.5, 0.09375, ((0, 4), (1, 8)))
    up_weight = scatter_about(seeds[3], (D, FF), D ** -0.5, 0.09375, ((0, 4), (1, 8)))
    dense_weight = scatter_about(seeds[4], (D, D), D ** -0.5, 0.09375, ((0, 8), (1, 4)))
    down_weight = scatter_about(seeds[5], (FF, D), FF ** -0.5, 0.046875, ((0, 8), (1, 4)))
    next_weight = scatter_about(seeds[6], (D, 3 * D), D ** -0.5, 0.09375, ((0, 4), (1, 8)))
    cache_keys = draw_cache_keys(jax.random.fold_in(seeds[12], 71), 0)
    cache_values = scatter_about(seeds[8], (SLOTS, PAGE, D), 1.0, 6.0, ((0, 4), (2, 8)))
    lengths = draw_lengths(jax.random.fold_in(seeds[12], 71), 0)
    slot_table = draw_slot_table(jax.random.fold_in(seeds[12], 71), 0)
    parents = set_ends(jax.random.randint(seeds[11], (STEPS - 1, BEAMS), 0, BEAM), jax.random.fold_in(seeds[11], 1), 0, BEAM - 1).astype(jnp.int32)
    return dict(inputs=inputs, norm_gains=norm_gains, attn_weight=attn_weight, up_weight=up_weight, dense_weight=dense_weight, down_weight=down_weight, next_weight=next_weight, cache_keys=cache_keys, cache_values=cache_values, lengths=lengths, slot_table=slot_table, parents=parents)


NEG_FILL = -1e+30
EPSILON = 1e-05

def normalize(block):
    values = block.astype(jnp.float32)
    row_mean = lax.optimization_barrier(jnp.mean(values, axis=1, keepdims=True))
    centred = values - row_mean
    row_var = lax.optimization_barrier(jnp.mean(centred * centred, axis=1, keepdims=True))
    return centred * lax.rsqrt(row_var + EPSILON)

def rotate(vectors, positions):
    half = ROT // 2
    freq = jnp.exp(jnp.arange(half, dtype=jnp.float32) * (-2.0 * math.log(10000.0) / ROT))
    angles = positions.astype(jnp.float32)[:, None] * freq[None, :]
    cosine = jnp.concatenate([jnp.cos(angles), jnp.cos(angles)], axis=1)[:, None, :]
    sine = jnp.concatenate([jnp.sin(angles), jnp.sin(angles)], axis=1)[:, None, :]
    turned = vectors[..., :ROT]
    swapped = jnp.concatenate([-turned[..., half:], turned[..., :half]], axis=-1)
    return jnp.concatenate([turned * cosine + swapped * sine, vectors[..., ROT:]], axis=-1)

def reference(inputs, norm_gains, attn_weight, up_weight, dense_weight, down_weight, next_weight, cache_keys, cache_values, lengths, slot_table, parents):
    scale = 1.0 / math.sqrt(HD)
    highest = lax.Precision.HIGHEST
    slot_owner = slot_table[0]
    slot_pageno = slot_table[1]
    valid_owner = jnp.maximum(slot_owner, 0)
    token_pos = slot_pageno[:, None] * PAGE + jnp.arange(PAGE, dtype=jnp.int32)[None, :]
    live = (slot_owner[:, None] >= 0) & (token_pos < lengths[valid_owner][:, None])
    owner_mask = slot_owner[:, None] == jnp.arange(REQUESTS, dtype=jnp.int32)[None, :]
    owner_float = owner_mask.astype(jnp.float32)
    gather_rows = valid_owner[:, None] * BEAM + jnp.arange(BEAM, dtype=jnp.int32)[None, :]
    beam_group = jnp.arange(BEAMS, dtype=jnp.int32) // BEAM
    tail_keys = jnp.zeros((STEPS, BEAMS, HEADS, HD), jnp.bfloat16)
    tail_values = jnp.zeros((STEPS, BEAMS, HEADS, HD), jnp.bfloat16)
    layer_list = []
    next_list = []
    for step_index in range(STEPS):
        if step_index > 0:
            source = (beam_group * BEAM + parents[step_index - 1]).astype(jnp.int32)
            tail_keys = tail_keys[:, source]
            tail_values = tail_values[:, source]
        block = inputs[step_index]
        normed = normalize(block)
        attn_in = (normed * norm_gains[0]).astype(jnp.bfloat16)
        mlp_in = (normed * norm_gains[1]).astype(jnp.bfloat16)
        mixed_qkv = jnp.dot(attn_in, attn_weight, preferred_element_type=jnp.float32).reshape(BEAMS, HEADS, 3, HD)
        hidden = jnp.dot(mlp_in, up_weight, preferred_element_type=jnp.float32)
        activated = jax.nn.gelu(hidden, approximate=False).astype(jnp.bfloat16)
        positions = lengths[beam_group] + step_index
        queries = rotate(mixed_qkv[:, :, 0], positions).astype(jnp.bfloat16)
        keys_new = rotate(mixed_qkv[:, :, 1], positions).astype(jnp.bfloat16)
        values_new = mixed_qkv[:, :, 2].astype(jnp.bfloat16)
        history_keys = jnp.concatenate([tail_keys[:step_index], keys_new[None]], axis=0)
        history_values = jnp.concatenate([tail_values[:step_index], values_new[None]], axis=0)

        def one_head(head):
            query = lax.dynamic_index_in_dim(queries, head, 1, keepdims=False).astype(jnp.float32)
            page_keys = lax.dynamic_slice_in_dim(cache_keys, head * HD, HD, 2).astype(jnp.float32)
            page_vals = lax.dynamic_slice_in_dim(cache_values, head * HD, HD, 2).astype(jnp.float32)
            chosen = query[gather_rows]
            scores = jnp.einsum('sbd,std->sbt', chosen, page_keys, precision=highest) * scale
            masked = jnp.where(live[:, None, :], scores, NEG_FILL)
            slot_top = lax.optimization_barrier(jnp.max(masked, axis=2))
            request_top = lax.optimization_barrier(jnp.max(jnp.where(owner_mask[:, :, None], slot_top[:, None, :], NEG_FILL), axis=0)).reshape(BEAMS)
            own_keys = lax.dynamic_index_in_dim(history_keys, head, 2, keepdims=False).astype(jnp.float32)
            own_vals = lax.dynamic_index_in_dim(history_values, head, 2, keepdims=False).astype(jnp.float32)
            own_scores = jnp.einsum('bd,nbd->bn', query, own_keys, precision=highest) * scale
            top = jnp.maximum(request_top, lax.optimization_barrier(jnp.max(own_scores, axis=1)))
            slot_ref = top.reshape(REQUESTS, BEAM)[valid_owner]
            weights = jnp.where(live[:, None, :], jnp.exp(masked - slot_ref[:, :, None]), 0.0)
            rounded = lax.optimization_barrier(weights.astype(jnp.bfloat16)).astype(jnp.float32)
            slot_out = jnp.einsum('sbt,std->sbd', rounded, page_vals, precision=highest)
            total = jnp.einsum('sr,sb->rb', owner_float, lax.optimization_barrier(jnp.sum(weights, axis=2)), precision=highest).reshape(BEAMS)
            summed = jnp.einsum('sr,sbd->rbd', owner_float, slot_out, precision=highest).reshape(BEAMS, HD)
            own_weights = jnp.exp(own_scores - top[:, None])
            own_rounded = lax.optimization_barrier(own_weights.astype(jnp.bfloat16)).astype(jnp.float32)
            total = total + lax.optimization_barrier(jnp.sum(own_weights, axis=1))
            summed = summed + jnp.einsum('bn,nbd->bd', own_rounded, own_vals, precision=highest)
            return summed / total[:, None]
        heads_out = lax.map(one_head, jnp.arange(HEADS, dtype=jnp.int32))
        attended = jnp.transpose(heads_out, (1, 0, 2)).reshape(BEAMS, D).astype(jnp.bfloat16)
        update = jnp.dot(attended, dense_weight, preferred_element_type=jnp.float32) + jnp.dot(activated, down_weight, preferred_element_type=jnp.float32)
        layer = (block.astype(jnp.float32) + update).astype(jnp.bfloat16)
        next_in = (normalize(layer) * norm_gains[2]).astype(jnp.bfloat16)
        next_out = jnp.dot(next_in, next_weight, preferred_element_type=jnp.float32).astype(jnp.bfloat16)
        tail_keys = tail_keys.at[step_index].set(keys_new)
        tail_values = tail_values.at[step_index].set(values_new)
        layer_list.append(layer)
        next_list.append(next_out)
    return (jnp.stack(layer_list), jnp.stack(next_list))
```

```python
import functools
import math

import jax
import jax.numpy as jnp
from jax import lax
from jax.experimental import pallas as pl
from jax.experimental.pallas import tpu as pltpu
from jax.sharding import PartitionSpec as P

HD = 128
ROT = 32
PAGE = 128
BEAM = 8
STEPS = 2
LANES = 128
STAT_ROWS = 16
GROUP = 8

NEG_FILL = -1e30
EPSILON = 1e-05
F32 = jnp.float32
BF16 = jnp.bfloat16


def rotated(array, axis, distance):
    size = lax.axis_size(axis)
    return lax.ppermute(array, axis, [(k, (k + distance) % size) for k in range(size)])


def flipped(array, axis, bits):
    return lax.ppermute(array, axis, [(k, k ^ bits) for k in range(lax.axis_size(axis))])


def gather_rows(block):
    size = lax.axis_size("mlp")
    me = lax.axis_index("mlp")
    pair, core = me // 2, me % 2
    pairs = size // 2
    near = [block] + [flipped(block, "mlp", 2 * d) for d in range(1, pairs)]
    near = jnp.stack(near)
    far = flipped(near, "mlp", 1)
    order = pair ^ jnp.arange(pairs)
    near, far = near[order], far[order]
    first = jnp.where(core == 0, near, far)
    second = jnp.where(core == 0, far, near)
    return jnp.stack([first, second], axis=1).reshape((size,) + block.shape)


def scatter_rows(partial):
    size = lax.axis_size("mlp")
    me = lax.axis_index("mlp")
    pair, core = me // 2, me % 2
    pairs = size // 2
    split = partial.reshape((pairs, 2) + partial.shape[1:])
    mine = lax.dynamic_index_in_dim(split, core, 1, keepdims=False)
    other = lax.dynamic_index_in_dim(split, 1 - core, 1, keepdims=False)
    summed = (mine.astype(F32) + flipped(other, "mlp", 1).astype(F32)).astype(BF16)
    total = lax.dynamic_index_in_dim(summed, pair, 0, keepdims=False).astype(F32)
    for d in range(1, pairs):
        piece = lax.dynamic_index_in_dim(summed, pair ^ d, 0, keepdims=False)
        total = total + flipped(piece, "mlp", 2 * d).astype(F32)
    return total


def row_statistics(values):
    size = lax.axis_size("req")
    width = values.shape[1]
    part_mean = jnp.mean(values, axis=1)
    part_square = jnp.sum(jnp.square(values - part_mean[:, None]), axis=1)
    packed = jnp.stack([part_mean, part_square]).reshape(2, -1, LANES)
    parts = jnp.stack([packed] + [rotated(packed, "req", d) for d in range(1, size)])
    mean = jnp.mean(parts[:, 0], axis=0)
    square = jnp.sum(parts[:, 1] + width * jnp.square(parts[:, 0] - mean), axis=0)
    scale = lax.rsqrt(square / (width * size) + EPSILON)
    return mean.reshape(-1, 1), scale.reshape(-1, 1)


def rotary_tables(positions):
    lane = jnp.arange(HD, dtype=jnp.int32)[None, :]
    half = ROT // 2
    freq = jnp.exp((lane % half).astype(F32) * (-2.0 * math.log(10000.0) / ROT))
    angles = positions.astype(F32)[:, None] * freq
    cosine = jnp.where(lane < ROT, jnp.cos(angles), 1.0)
    sine = jnp.sin(angles)
    upper = jnp.where(lane < half, -sine, 0.0)
    lower = jnp.where((lane >= half) & (lane < ROT), sine, 0.0)
    return cosine, upper, lower


def full_block(shape):
    return pl.BlockSpec(shape, lambda *_: (0,) * len(shape))


def head_split_kernel(heads, parts, requests, x_ref, c_ref, u_ref, l_ref, q_ref, k_ref, v_ref):
    rows = requests * BEAM
    for head in range(heads):
        for kind, out in enumerate((q_ref, k_ref, v_ref)):
            column = (head * 3 + kind) * HD
            value = x_ref[:, column : column + HD].astype(F32)
            if kind < 2:
                value = (
                    value * c_ref[...]
                    + pltpu.roll(value, HD - ROT // 2, 1) * u_ref[...]
                    + pltpu.roll(value, ROT // 2, 1) * l_ref[...]
                )
            for part in range(parts):
                for request in range(requests):
                    first = part * STEPS * rows + request * BEAM
                    pair = [value[first + s * rows : first + s * rows + BEAM] for s in range(STEPS)]
                    at = ((part * requests + request) * heads + head) * STEPS * BEAM
                    out[at : at + STEPS * BEAM, :] = jnp.concatenate(pair, axis=0).astype(BF16)


def head_split(shared, tables, heads, parts, requests):
    rows = parts * requests * heads * STEPS * BEAM
    shape = jax.ShapeDtypeStruct((rows, HD), BF16)
    return pl.pallas_call(
        functools.partial(head_split_kernel, heads, parts, requests),
        out_shape=(shape, shape, shape),
        compiler_params=pltpu.CompilerParams(vmem_limit_bytes=32 << 20),
    )(shared, *tables)


def page_kernel(heads, ranks, own_rows, slot_ref, length_ref, me_ref, q_ref, k_ref, v_ref, *rest):
    outs, (top_ref, sum_ref, out_ref) = rest[:ranks], rest[ranks:]
    step = pl.program_id(0)
    height = heads * STEPS * BEAM
    chunk = STEPS * BEAM
    scale = 1.0 / math.sqrt(HD)

    @pl.when(step == 0)
    def _():
        top_ref[...] = jnp.full(top_ref.shape, NEG_FILL, F32)
        sum_ref[...] = jnp.zeros(sum_ref.shape, F32)
        out_ref[...] = jnp.zeros(out_ref.shape, F32)

    lane = lax.broadcasted_iota(jnp.int32, (height, PAGE), 1)
    found = []
    for g in range(GROUP):
        slot = step * GROUP + g
        owner = slot_ref[0, slot]
        valid = jnp.maximum(owner, 0)
        limit = jnp.where(owner >= 0, length_ref[valid] - slot_ref[1, slot] * PAGE, 0)
        base = pl.multiple_of(valid * height, height)
        scores = []
        for h in range(heads):
            query = q_ref[pl.ds(pl.multiple_of(base + h * chunk, chunk), chunk), :]
            key = k_ref[g, :, h * HD : (h + 1) * HD]
            scores.append(
                lax.dot_general(query, key, (((1,), (1,)), ((), ())), preferred_element_type=F32)
            )
        live = lane < limit
        score = jnp.where(live, jnp.concatenate(scores, axis=0) * scale, NEG_FILL)
        top = jnp.max(score, axis=1, keepdims=True)
        weight = jnp.where(live, jnp.exp(score - top), 0.0)
        total = jnp.sum(weight, axis=1, keepdims=True)
        weight = weight.astype(BF16)
        value = [
            jnp.dot(
                weight[h * chunk : (h + 1) * chunk],
                v_ref[g, :, h * HD : (h + 1) * HD],
                preferred_element_type=F32,
            )
            for h in range(heads)
        ]
        found.append((base, top, total, jnp.concatenate(value, axis=0)))
    for base, top, total, value in found:
        at = pl.ds(base, height)
        old = top_ref[at, :]
        new = jnp.maximum(old, top)
        left = jnp.exp(old - new)
        right = jnp.exp(top - new)
        top_ref[at, :] = new
        sum_ref[at, :] = sum_ref[at, :] * left + total * right
        out_ref[at, :] = out_ref[at, :] * left + value * right

    @pl.when(step == pl.num_programs(0) - 1)
    def _():
        eye = lax.broadcasted_iota(jnp.int32, (LANES, LANES), 0) == lax.broadcasted_iota(
            jnp.int32, (LANES, LANES), 1
        )
        blocks = own_rows // LANES
        for d in range(ranks):
            rank = lax.rem(me_ref[0] + d, ranks)
            levels = []
            for block in range(blocks):
                first = pl.multiple_of(rank * own_rows + block * LANES, LANES)
                total = sum_ref[pl.ds(first, LANES), :]
                some = total > 0.0
                total = jnp.where(some, total, 1.0)
                outs[d][block * LANES : (block + 1) * LANES, :] = (
                    out_ref[pl.ds(first, LANES), :] / total
                ).astype(BF16)
                level = jnp.where(some, top_ref[pl.ds(first, LANES), :] + jnp.log(total), NEG_FILL)
                levels.append(jnp.sum(jnp.where(eye, level, 0.0), axis=0, keepdims=True))
            levels.append(jnp.zeros((STAT_ROWS - blocks, LANES), F32))
            level = jnp.concatenate(levels, axis=0)
            for k in range(3):
                rounded = level.astype(BF16)
                level = level - rounded.astype(F32)
                outs[d][own_rows + k * STAT_ROWS : own_rows + (k + 1) * STAT_ROWS, :] = rounded


def page_attention(queries, keys, values, slot_table, lengths, heads, ranks):
    slots = keys.shape[0]
    rows = queries.shape[0]
    own_rows = rows // ranks
    me = lax.axis_index("req").astype(jnp.int32).reshape(1)
    out_rows = own_rows + 3 * STAT_ROWS
    shape = jax.ShapeDtypeStruct((out_rows, LANES), BF16)
    page_block = pl.BlockSpec((GROUP, PAGE, heads * HD), lambda g, *_: (g, 0, 0))
    return pl.pallas_call(
        functools.partial(page_kernel, heads, ranks, own_rows),
        out_shape=(shape,) * ranks,
        grid_spec=pltpu.PrefetchScalarGridSpec(
            num_scalar_prefetch=3,
            grid=(slots // GROUP,),
            in_specs=[full_block((rows, HD)), page_block, page_block],
            out_specs=[full_block((out_rows, LANES))] * ranks,
            scratch_shapes=[pltpu.VMEM((rows, LANES), F32)] * 3,
        ),
        compiler_params=pltpu.CompilerParams(vmem_limit_bytes=40 << 20),
        cost_estimate=pl.CostEstimate(
            flops=4 * slots * PAGE * heads * HD * STEPS * BEAM,
            bytes_accessed=2 * slots * PAGE * heads * HD * 2,
            transcendentals=slots * PAGE * heads * STEPS * BEAM,
        ),
    )(slot_table, lengths, me, queries, keys, values)


def merge_kernel(heads, ranks, parts, requests, q_ref, k_ref, v_ref, parent_ref, *rest):
    pieces, out, work = rest[:ranks], rest[ranks], rest[ranks + 1]
    chunk = STEPS * BEAM
    height = heads * chunk
    own_rows = q_ref.shape[0]
    scale = 1.0 / math.sqrt(HD)
    eye = lax.broadcasted_iota(jnp.int32, (LANES, LANES), 0) == lax.broadcasted_iota(
        jnp.int32, (LANES, LANES), 1
    )
    late = lax.broadcasted_iota(jnp.int32, (LANES, 1), 0) % chunk >= BEAM
    levels = []
    for piece in pieces:
        level = jnp.zeros((STAT_ROWS, LANES), F32)
        for k in range(3):
            first = own_rows + k * STAT_ROWS
            level = level + piece[first : first + STAT_ROWS, :].astype(F32)
        levels.append(level)
    for block in range(own_rows // LANES):
        at = slice(block * LANES, (block + 1) * LANES)
        query = q_ref[at, :].astype(F32)
        key = k_ref[at, :].astype(F32)
        value = v_ref[at, :].astype(F32)
        held_keys, held_values = [], []
        for tile in range(LANES // chunk):
            first = tile * chunk
            request = (block * LANES + first) // height
            parent = parent_ref[request * BEAM : (request + 1) * BEAM, :]
            for held, source in ((held_keys, key), (held_values, value)):
                chosen = jnp.zeros((BEAM, HD), F32)
                for beam in range(BEAM):
                    row = source[first + beam : first + beam + 1, :]
                    chosen = jnp.where(parent == beam, row, chosen)
                held += [jnp.zeros((BEAM, HD), F32), chosen]
        held_key = jnp.concatenate(held_keys, axis=0)
        held_value = jnp.concatenate(held_values, axis=0)
        own = jnp.sum(query * key, axis=1, keepdims=True) * scale
        past = jnp.sum(query * held_key, axis=1, keepdims=True) * scale
        past = jnp.where(late, past, NEG_FILL)
        columns = [
            jnp.sum(jnp.where(eye, level[block : block + 1, :], 0.0), axis=1, keepdims=True)
            for level in levels
        ]
        top = functools.reduce(jnp.maximum, columns, jnp.maximum(own, past))
        own = jnp.exp(own - top)
        past = jnp.where(late, jnp.exp(past - top), 0.0)
        total = own + past
        result = own * value + past * held_value
        for column, piece in zip(columns, pieces):
            factor = jnp.exp(column - top)
            total = total + factor
            result = result + factor * piece[at, :].astype(F32)
        work[at, :] = result / total
    rows = requests * BEAM
    for part in range(parts):
        for request in range(0, requests, 2):
            for head in range(heads):
                for s in range(STEPS):
                    tiles = []
                    for r in (request, request + 1):
                        first = (part * requests + r) * height + head * chunk + s * BEAM
                        tiles.append(work[first : first + BEAM, :])
                    first = (part * STEPS + s) * rows + request * BEAM
                    out[first : first + 2 * BEAM, head * HD : (head + 1) * HD] = jnp.concatenate(
                        tiles, axis=0
                    ).astype(BF16)


def merge(queries, keys, values, parents, pieces, heads, parts, requests):
    ranks = len(pieces)
    rows = parts * requests * STEPS * BEAM
    return pl.pallas_call(
        functools.partial(merge_kernel, heads, ranks, parts, requests),
        out_shape=jax.ShapeDtypeStruct((rows, heads * HD), BF16),
        scratch_shapes=[pltpu.VMEM(queries.shape, F32)],
        compiler_params=pltpu.CompilerParams(vmem_limit_bytes=32 << 20),
    )(queries, keys, values, parents, *pieces)


def shards(
    inputs,
    norm_gains,
    attn_weight,
    up_weight,
    dense_weight,
    down_weight,
    next_weight,
    cache_keys,
    cache_values,
    lengths,
    slot_table,
    parents,
):
    ranks = lax.axis_size("req")
    parts = lax.axis_size("mlp") // ranks
    own_count = parents.shape[1]
    beams = inputs.shape[1]
    width = inputs.shape[2]
    requests = beams // BEAM
    own_requests = own_count // BEAM
    heads = dense_weight.shape[0] // HD
    rank = lax.axis_index("req")

    own_lengths = lax.dynamic_slice_in_dim(lengths, rank * own_requests, own_requests, 0)
    positions = jnp.broadcast_to(
        own_lengths.reshape(parts, 1, requests, 1)
        + jnp.arange(STEPS, dtype=jnp.int32).reshape(1, STEPS, 1, 1),
        (parts, STEPS, requests, BEAM),
    ).reshape(-1)
    tables = rotary_tables(positions)
    parent_wide = jnp.broadcast_to(parents[0][:, None], (own_count, LANES))

    block = inputs.reshape(STEPS * beams, width)
    with jax.named_scope("gather_inputs"):
        everything = gather_rows(block).reshape(-1, width).astype(F32)
    with jax.named_scope("norm"):
        mean, scale = row_statistics(everything)
        normed = (everything - mean) * scale
        attn_in = (normed * norm_gains[0]).astype(BF16)
        mlp_in = (normed * norm_gains[1]).astype(BF16)
    with jax.named_scope("qkv"):
        mixed = jnp.dot(attn_in, attn_weight, preferred_element_type=F32).astype(BF16)
        mixed = lax.psum_scatter(mixed, "req", scatter_dimension=0, tiled=True)
    with jax.named_scope("up"):
        hidden = jnp.dot(mlp_in, up_weight, preferred_element_type=F32).astype(BF16)
        hidden = lax.psum_scatter(hidden, "req", scatter_dimension=0, tiled=True).astype(F32)
        activated = jax.nn.gelu(hidden, approximate=False).astype(BF16)
        activated = lax.all_gather(activated, "req", axis=0, tiled=True)
    with jax.named_scope("attention"):
        queries, keys, values = head_split(mixed, tables, heads, parts, requests)
        queries_all = lax.all_gather(queries, "req", axis=0, tiled=True)
        pieces = page_attention(
            queries_all, cache_keys, cache_values, slot_table, lengths, heads, ranks
        )
        pieces = [pieces[0]] + [rotated(pieces[d], "req", d) for d in range(1, ranks)]
        attended = merge(queries, keys, values, parent_wide, pieces, heads, parts, requests)
        attended = lax.all_gather(attended, "req", axis=0, tiled=True)
    with jax.named_scope("down"):
        update = jnp.dot(attended, dense_weight, preferred_element_type=F32) + jnp.dot(
            activated, down_weight, preferred_element_type=F32
        )
        update = scatter_rows(update.astype(BF16).reshape(-1, STEPS * beams, width))
        layer = (block.astype(F32) + update).astype(BF16)
    with jax.named_scope("next"):
        everything = gather_rows(layer).reshape(-1, width).astype(F32)
        mean, scale = row_statistics(everything)
        next_in = ((everything - mean) * scale * norm_gains[2]).astype(BF16)
        following = jnp.dot(next_in, next_weight, preferred_element_type=F32).astype(BF16)
        following = lax.psum_scatter(following, "req", scatter_dimension=0, tiled=True)
        following = following.reshape(parts, STEPS, beams, -1).transpose(1, 0, 2, 3)
    return layer.reshape(STEPS, beams, width), following.reshape(STEPS, own_count, -1)


def solution(mesh):
    in_specs = (
        P(None, "mlp", "req"),
        P(None, "req"),
        P("req", "mlp"),
        P("req", "mlp"),
        P("mlp", "req"),
        P("mlp", "req"),
        P("req", "mlp"),
        P("req", None, "mlp"),
        P("req", None, "mlp"),
        P(),
        P(None, "req"),
        P(None, "req"),
    )
    out_specs = (P(None, "mlp", "req"), P(None, "req", "mlp"))
    return jax.shard_map(shards, mesh=mesh, in_specs=in_specs, out_specs=out_specs, check_vma=False)
```

```python
import functools
import math

import jax
import jax.numpy as jnp
from jax import lax
from jax.experimental import pallas as pl
from jax.experimental.pallas import tpu as pltpu
from jax.sharding import PartitionSpec as P

HD = 128
ROT = 32
PAGE = 128
BEAM = 8
STEPS = 2
LANES = 128
STAT_ROWS = 16
GROUP = 8

NEG_FILL = -1e30
EPSILON = 1e-05
F32 = jnp.float32
BF16 = jnp.bfloat16


def rotated(array, axis, distance):
    size = lax.axis_size(axis)
    return lax.ppermute(array, axis, [(k, (k + distance) % size) for k in range(size)])


def flipped(array, axis, bits):
    return lax.ppermute(array, axis, [(k, k ^ bits) for k in range(lax.axis_size(axis))])


def gather_pieces(block):
    pairs = lax.axis_size("mlp") // 2
    near = [block] + [flipped(block, "mlp", 2 * d) for d in range(1, pairs)]
    far = [flipped(piece, "mlp", 1) for piece in near]
    return near + far


def scatter_sum(mine, other):
    size = lax.axis_size("req")
    pair = lax.axis_index("mlp") // 2
    rank = lax.axis_index("req")
    summed = (mine.astype(F32) + flipped(other, "mlp", 1).astype(F32)).astype(BF16)

    def block(owner):
        return lax.dynamic_index_in_dim(summed, (rank - owner) % size, 0, keepdims=False)

    total = block(pair).astype(F32)
    for d in range(1, size):
        total = total + flipped(block(pair ^ d), "mlp", 2 * d).astype(F32)
    return total


def line_scatter(partial):
    size = lax.axis_size("req")
    rank = lax.axis_index("req")

    def block(owner):
        return lax.dynamic_index_in_dim(
            partial, jnp.clip(owner, 0, size - 1), 0, keepdims=False
        ).astype(F32)

    right = left = None
    for t in range(1, size):
        to_right, to_left = block(rank + size - t), block(rank - size + t)
        if right is not None:
            to_right, to_left = to_right + right, to_left + left
        right = lax.ppermute(to_right.astype(BF16), "req", [(k, k + 1) for k in range(t)])
        left = lax.ppermute(
            to_left.astype(BF16), "req", [(size - 1 - k, size - 2 - k) for k in range(t)]
        )
        right, left = right.astype(F32), left.astype(F32)
    return block(rank) + right + left


def line_gather(block):
    size = lax.axis_size("req")
    rights, lefts = [], []
    right = left = block
    for t in range(1, size):
        right = lax.ppermute(right, "req", [(k, k + 1) for k in range(t - 1, size - 1)])
        left = lax.ppermute(left, "req", [(k + 1, k) for k in range(size - t)])
        rights.append(right)
        lefts.append(left)
    return rights, lefts


def eye_mask(rows):
    shape = (rows, LANES)
    return lax.broadcasted_iota(jnp.int32, shape, 0) == lax.broadcasted_iota(jnp.int32, shape, 1)


def project_kernel(count, steps, place_ref, gain_ref, weight_ref, *refs):
    pieces, (out, stats, *extra, held) = refs[:count], refs[count:]
    rows = pieces[0].shape[0]
    beams = rows // steps

    @pl.when(pl.program_id(0) == 0)
    def _():
        eye = eye_mask(rows)
        pair, core = place_ref[0] // 2, place_ref[0] % 2
        for k in range(count):
            d, away = k % (count // 2), k // (count // 2)
            owner = (pair ^ d) * 2 + (core ^ away)
            value = pieces[k][...].astype(F32)
            mean = jnp.mean(value, axis=1, keepdims=True)
            centred = value - mean
            square = jnp.sum(centred * centred, axis=1, keepdims=True)
            for row, column in ((owner, mean), (count + owner, square)):
                stats[pl.ds(row, 1), :] = jnp.sum(
                    jnp.where(eye, column, 0.0), axis=0, keepdims=True
                )
            at = pl.ds(pl.multiple_of(owner * rows, rows), rows)
            held[at, :] = (centred * gain_ref[0:1, :]).astype(BF16)
            if extra:
                scaled = (centred * gain_ref[1:2, :]).astype(BF16)
                at = pl.ds(pl.multiple_of(owner * beams, beams), beams)
                for s in range(steps):
                    extra[s][at, :] = scaled[s * beams : (s + 1) * beams]

    out[...] = jnp.dot(held[...], weight_ref[...], preferred_element_type=F32).astype(BF16)


def project(pieces, gains, weight, steps):
    count = len(pieces)
    rows, width = pieces[0].shape
    columns = weight.shape[1]
    tile = math.gcd(columns, 256)
    place = lax.axis_index("mlp").astype(jnp.int32).reshape(1)
    extra = jax.ShapeDtypeStruct((count * rows // steps, width), BF16)
    extras = (extra,) * (steps if gains.shape[0] > 1 else 0)
    stats = jax.ShapeDtypeStruct((2 * count, LANES), F32)
    return pl.pallas_call(
        functools.partial(project_kernel, count, steps),
        out_shape=(jax.ShapeDtypeStruct((count * rows, columns), BF16), stats) + extras,
        grid=(columns // tile,),
        in_specs=[
            pl.BlockSpec(memory_space=pltpu.SMEM),
            full_block(gains.shape),
            pl.BlockSpec((width, tile), lambda n: (0, n)),
        ]
        + [full_block((rows, width))] * count,
        out_specs=[pl.BlockSpec((count * rows, tile), lambda n: (0, n)), full_block(stats.shape)]
        + [full_block(extra.shape)] * len(extras),
        scratch_shapes=[pltpu.VMEM((count * rows, width), BF16)],
        compiler_params=pltpu.CompilerParams(vmem_limit_bytes=32 << 20),
        cost_estimate=pl.CostEstimate(
            flops=2 * count * rows * width * columns,
            bytes_accessed=2 * (width * columns + count * rows * (2 * width + columns)),
            transcendentals=0,
        ),
    )(place, gains, weight, *pieces)


def exchange(part):
    return [part] + [rotated(part, "req", d) for d in range(1, lax.axis_size("req"))]


def own_statistics(stats, width, rows):
    size = lax.axis_size("req")
    count = stats.shape[0] // 2
    parts = jnp.stack(exchange(stats)).reshape(size, 2, count, LANES)
    parts = lax.dynamic_slice_in_dim(parts, 2 * lax.axis_index("req"), 2, 2)[..., :rows]
    mean = jnp.mean(parts[:, 0], axis=0)
    away = parts[:, 0] - mean
    square = jnp.sum(parts[:, 1] + width * jnp.square(away), axis=0)
    return away, lax.rsqrt(square / (width * size) + EPSILON)


def weight_sums(gain, weight):
    high = gain.astype(BF16)
    low = (gain - high.astype(F32)).astype(BF16)
    rows = jnp.zeros((16, gain.shape[0]), BF16).at[0].set(high).at[1].set(low)
    both = jnp.dot(rows, weight, preferred_element_type=F32)
    return both[0] + both[1]


def corrected(total, away, scale, sums):
    for part, columns in zip(away, sums):
        total = total + part.reshape(-1, 1) * columns[None, :]
    return total * scale.reshape(-1, 1)


def update_kernel(ranks, steps, step, place_ref, down_ref, dense_ref, *refs):
    attended, refs = refs[:ranks], refs[ranks:]
    own, rights, lefts = refs[0], refs[1:ranks], refs[ranks : 2 * ranks - 1]
    mine, other, hidden, heads = refs[2 * ranks - 1 :]
    rows = own.shape[0]
    rank, core = place_ref[0], place_ref[1]

    @pl.when(pl.program_id(0) == 0)
    def _():
        hidden[0:rows, :] = own[...]
        for d in range(1, ranks):
            at = slice(d * rows, (d + 1) * rows)

            @pl.when(rank >= d)
            def _():
                hidden[at, :] = rights[d - 1][...]

            @pl.when(rank < d)
            def _():
                hidden[at, :] = lefts[ranks - d - 1][...]

        for d in range(ranks):
            heads[d * rows : (d + 1) * rows, :] = attended[d][step * rows : (step + 1) * rows, :]

    result = jnp.dot(hidden[...], down_ref[...], preferred_element_type=F32) + jnp.dot(
        heads[...], dense_ref[...], preferred_element_type=F32
    )
    half = rows // 2
    for d in range(ranks):
        first = result[d * rows : d * rows + half]
        second = result[d * rows + half : (d + 1) * rows]
        mine[d] = jnp.where(core == 0, first, second).astype(BF16)
        other[d] = jnp.where(core == 0, second, first).astype(BF16)


def layer_update(step, attended, own, rights, lefts, dense_weight, down_weight):
    ranks = lax.axis_size("req")
    rows, hidden = own.shape
    head_width, width = dense_weight.shape
    tile = min(256, width)
    place = jnp.stack([lax.axis_index("req"), lax.axis_index("mlp") % 2]).astype(jnp.int32)
    shape = jax.ShapeDtypeStruct((ranks, rows // 2, width), BF16)
    out_block = pl.BlockSpec((ranks, rows // 2, tile), lambda n: (0, 0, n))
    return pl.pallas_call(
        functools.partial(update_kernel, ranks, STEPS, step),
        out_shape=(shape, shape),
        grid=(width // tile,),
        in_specs=[
            pl.BlockSpec(memory_space=pltpu.SMEM),
            pl.BlockSpec((hidden, tile), lambda n: (0, n)),
            pl.BlockSpec((head_width, tile), lambda n: (0, n)),
        ]
        + [full_block(attended[0].shape)] * ranks
        + [full_block((rows, hidden))] * (2 * ranks - 1),
        out_specs=(out_block, out_block),
        scratch_shapes=[
            pltpu.VMEM((ranks * rows, hidden), BF16),
            pltpu.VMEM((ranks * rows, head_width), BF16),
        ],
        compiler_params=pltpu.CompilerParams(vmem_limit_bytes=40 << 20),
        cost_estimate=pl.CostEstimate(
            flops=2 * ranks * rows * (hidden + head_width) * width,
            bytes_accessed=2 * (hidden + head_width) * width + 4 * ranks * rows * hidden,
            transcendentals=0,
        ),
    )(place, down_weight, dense_weight, *attended, own, *rights, *lefts)


def rotary_tables(positions):
    lane = jnp.arange(HD, dtype=jnp.int32)[None, :]
    half = ROT // 2
    freq = jnp.exp((lane % half).astype(F32) * (-2.0 * math.log(10000.0) / ROT))
    angles = positions.astype(F32)[:, None] * freq
    cosine = jnp.where(lane < ROT, jnp.cos(angles), 1.0)
    sine = jnp.sin(angles)
    upper = jnp.where(lane < half, -sine, 0.0)
    lower = jnp.where((lane >= half) & (lane < ROT), sine, 0.0)
    return cosine, upper, lower


def full_block(shape):
    return pl.BlockSpec(shape, lambda *_: (0,) * len(shape))


def head_split_kernel(heads, parts, requests, ranks, x_ref, stat_ref, sum_ref, *refs):
    tables, outs = refs[:3], refs[3:]
    rows = requests * BEAM
    scale = stat_ref[:, ranks : ranks + 1]
    for head in range(heads):
        for kind, out in enumerate(outs):
            column = (head * 3 + kind) * HD
            value = x_ref[:, column : column + HD].astype(F32)
            for d in range(ranks):
                value = value + stat_ref[:, d : d + 1] * sum_ref[d : d + 1, column : column + HD]
            value = value * scale
            if kind < 2:
                value = (
                    value * tables[0][...]
                    + pltpu.roll(value, HD - ROT // 2, 1) * tables[1][...]
                    + pltpu.roll(value, ROT // 2, 1) * tables[2][...]
                )
            for part in range(parts):
                for request in range(requests):
                    first = part * STEPS * rows + request * BEAM
                    pair = [value[first + s * rows : first + s * rows + BEAM] for s in range(STEPS)]
                    at = ((part * requests + request) * heads + head) * STEPS * BEAM
                    out[at : at + STEPS * BEAM, :] = jnp.concatenate(pair, axis=0).astype(BF16)


def head_split(shared, away, scale, sums, tables, heads, parts, requests):
    ranks = len(sums)
    stats = jnp.concatenate([away.reshape(ranks, -1), scale.reshape(1, -1)]).T
    stats = jnp.pad(stats, ((0, 0), (0, LANES - ranks - 1)))
    shape = jax.ShapeDtypeStruct((parts * requests * heads * STEPS * BEAM, HD), BF16)
    return pl.pallas_call(
        functools.partial(head_split_kernel, heads, parts, requests, ranks),
        out_shape=(shape, shape, shape),
        compiler_params=pltpu.CompilerParams(vmem_limit_bytes=32 << 20),
    )(shared, stats, jnp.stack(sums), *tables)


def page_kernel(heads, ranks, own_rows, slot_ref, length_ref, me_ref, k_ref, v_ref, *rest):
    queries, outs = rest[:ranks], rest[ranks : 2 * ranks]
    q_ref, top_ref, sum_ref, out_ref = rest[2 * ranks :]
    step = pl.program_id(0)
    height = heads * STEPS * BEAM
    chunk = STEPS * BEAM
    scale = 1.0 / math.sqrt(HD)

    @pl.when(step == 0)
    def _():
        for d in range(ranks):
            rank = lax.rem(me_ref[0] + ranks - d, ranks)
            q_ref[pl.ds(pl.multiple_of(rank * own_rows, own_rows), own_rows), :] = queries[d][...]
        top_ref[...] = jnp.full(top_ref.shape, NEG_FILL, F32)
        sum_ref[...] = jnp.zeros(sum_ref.shape, F32)
        out_ref[...] = jnp.zeros(out_ref.shape, F32)

    lane = lax.broadcasted_iota(jnp.int32, (height, PAGE), 1)
    found = []
    for g in range(GROUP):
        slot = step * GROUP + g
        owner = slot_ref[0, slot]
        valid = jnp.maximum(owner, 0)
        limit = jnp.where(owner >= 0, length_ref[valid] - slot_ref[1, slot] * PAGE, 0)
        base = pl.multiple_of(valid * height, height)
        scores = []
        for h in range(heads):
            query = q_ref[pl.ds(pl.multiple_of(base + h * chunk, chunk), chunk), :]
            key = k_ref[g, :, h * HD : (h + 1) * HD]
            scores.append(
                lax.dot_general(query, key, (((1,), (1,)), ((), ())), preferred_element_type=F32)
            )
        live = lane < limit
        score = jnp.where(live, jnp.concatenate(scores, axis=0) * scale, NEG_FILL)
        top = jnp.max(score, axis=1, keepdims=True)
        weight = jnp.where(live, jnp.exp(score - top), 0.0)
        total = jnp.sum(weight, axis=1, keepdims=True)
        weight = weight.astype(BF16)
        value = [
            jnp.dot(
                weight[h * chunk : (h + 1) * chunk],
                v_ref[g, :, h * HD : (h + 1) * HD],
                preferred_element_type=F32,
            )
            for h in range(heads)
        ]
        found.append((base, top, total, jnp.concatenate(value, axis=0)))
    for base, top, total, value in found:
        at = pl.ds(base, height)
        old = top_ref[at, :]
        new = jnp.maximum(old, top)
        left = jnp.exp(old - new)
        right = jnp.exp(top - new)
        top_ref[at, :] = new
        sum_ref[at, :] = sum_ref[at, :] * left + total * right
        out_ref[at, :] = out_ref[at, :] * left + value * right

    @pl.when(step == pl.num_programs(0) - 1)
    def _():
        eye = lax.broadcasted_iota(jnp.int32, (LANES, LANES), 0) == lax.broadcasted_iota(
            jnp.int32, (LANES, LANES), 1
        )
        blocks = own_rows // LANES
        for d in range(ranks):
            rank = lax.rem(me_ref[0] + d, ranks)
            levels = []
            for block in range(blocks):
                first = pl.multiple_of(rank * own_rows + block * LANES, LANES)
                total = sum_ref[pl.ds(first, LANES), :]
                some = total > 0.0
                total = jnp.where(some, total, 1.0)
                outs[d][block * LANES : (block + 1) * LANES, :] = (
                    out_ref[pl.ds(first, LANES), :] / total
                ).astype(BF16)
                level = jnp.where(some, top_ref[pl.ds(first, LANES), :] + jnp.log(total), NEG_FILL)
                levels.append(jnp.sum(jnp.where(eye, level, 0.0), axis=0, keepdims=True))
            levels.append(jnp.zeros((STAT_ROWS - blocks, LANES), F32))
            level = jnp.concatenate(levels, axis=0)
            for k in range(3):
                rounded = level.astype(BF16)
                level = level - rounded.astype(F32)
                outs[d][own_rows + k * STAT_ROWS : own_rows + (k + 1) * STAT_ROWS, :] = rounded


def page_attention(queries, keys, values, slot_table, lengths, heads, ranks):
    slots = keys.shape[0]
    own_rows = queries[0].shape[0]
    rows = own_rows * ranks
    me = lax.axis_index("req").astype(jnp.int32).reshape(1)
    out_rows = own_rows + 3 * STAT_ROWS
    shape = jax.ShapeDtypeStruct((out_rows, LANES), BF16)
    page_block = pl.BlockSpec((GROUP, PAGE, heads * HD), lambda g, *_: (g, 0, 0))
    return pl.pallas_call(
        functools.partial(page_kernel, heads, ranks, own_rows),
        out_shape=(shape,) * ranks,
        grid_spec=pltpu.PrefetchScalarGridSpec(
            num_scalar_prefetch=3,
            grid=(slots // GROUP,),
            in_specs=[page_block, page_block] + [full_block((own_rows, HD))] * ranks,
            out_specs=[full_block((out_rows, LANES))] * ranks,
            scratch_shapes=[pltpu.VMEM((rows, HD), BF16)] + [pltpu.VMEM((rows, LANES), F32)] * 3,
        ),
        compiler_params=pltpu.CompilerParams(vmem_limit_bytes=40 << 20),
        cost_estimate=pl.CostEstimate(
            flops=4 * slots * PAGE * heads * HD * STEPS * BEAM,
            bytes_accessed=2 * slots * PAGE * heads * HD * 2,
            transcendentals=slots * PAGE * heads * STEPS * BEAM,
        ),
    )(slot_table, lengths, me, keys, values, *queries)


def merge_kernel(heads, ranks, requests, q_ref, k_ref, v_ref, parent_ref, *rest):
    pieces, out, work = rest[:ranks], rest[ranks], rest[ranks + 1]
    chunk = STEPS * BEAM
    height = heads * chunk
    own_rows = q_ref.shape[0]
    scale = 1.0 / math.sqrt(HD)
    eye = lax.broadcasted_iota(jnp.int32, (LANES, LANES), 0) == lax.broadcasted_iota(
        jnp.int32, (LANES, LANES), 1
    )
    late = lax.broadcasted_iota(jnp.int32, (LANES, 1), 0) % chunk >= BEAM
    levels = []
    for piece in pieces:
        level = jnp.zeros((STAT_ROWS, LANES), F32)
        for k in range(3):
            first = own_rows + k * STAT_ROWS
            level = level + piece[first : first + STAT_ROWS, :].astype(F32)
        levels.append(level)
    for block in range(own_rows // LANES):
        at = slice(block * LANES, (block + 1) * LANES)
        query = q_ref[at, :].astype(F32)
        key = k_ref[at, :].astype(F32)
        value = v_ref[at, :].astype(F32)
        held_keys, held_values = [], []
        for tile in range(LANES // chunk):
            first = tile * chunk
            request = (block * LANES + first) // height
            parent = parent_ref[request * BEAM : (request + 1) * BEAM, :]
            for held, source in ((held_keys, key), (held_values, value)):
                chosen = jnp.zeros((BEAM, HD), F32)
                for beam in range(BEAM):
                    row = source[first + beam : first + beam + 1, :]
                    chosen = jnp.where(parent == beam, row, chosen)
                held += [jnp.zeros((BEAM, HD), F32), chosen]
        held_key = jnp.concatenate(held_keys, axis=0)
        held_value = jnp.concatenate(held_values, axis=0)
        own = jnp.sum(query * key, axis=1, keepdims=True) * scale
        past = jnp.sum(query * held_key, axis=1, keepdims=True) * scale
        past = jnp.where(late, past, NEG_FILL)
        columns = [
            jnp.sum(jnp.where(eye, level[block : block + 1, :], 0.0), axis=1, keepdims=True)
            for level in levels
        ]
        top = functools.reduce(jnp.maximum, columns, jnp.maximum(own, past))
        own = jnp.exp(own - top)
        past = jnp.where(late, jnp.exp(past - top), 0.0)
        total = own + past
        result = own * value + past * held_value
        for column, piece in zip(columns, pieces):
            factor = jnp.exp(column - top)
            total = total + factor
            result = result + factor * piece[at, :].astype(F32)
        work[at, :] = result / total
    rows = requests * BEAM
    for request in range(0, requests, 2):
        for head in range(heads):
            for s in range(STEPS):
                tiles = []
                for r in (request, request + 1):
                    first = r * height + head * chunk + s * BEAM
                    tiles.append(work[first : first + BEAM, :])
                first = s * rows + request * BEAM
                out[first : first + 2 * BEAM, head * HD : (head + 1) * HD] = jnp.concatenate(
                    tiles, axis=0
                ).astype(BF16)


def merge(queries, keys, values, parents, pieces, heads, requests):
    ranks = len(pieces)
    rows = requests * STEPS * BEAM
    return pl.pallas_call(
        functools.partial(merge_kernel, heads, ranks, requests),
        out_shape=jax.ShapeDtypeStruct((rows, heads * HD), BF16),
        scratch_shapes=[pltpu.VMEM(queries.shape, F32)],
        compiler_params=pltpu.CompilerParams(vmem_limit_bytes=32 << 20),
    )(queries, keys, values, parents, *pieces)


def shards(
    inputs,
    norm_gains,
    attn_weight,
    up_weight,
    dense_weight,
    down_weight,
    next_weight,
    cache_keys,
    cache_values,
    lengths,
    slot_table,
    parents,
):
    ranks = lax.axis_size("req")
    own_count = parents.shape[1]
    beams = inputs.shape[1]
    width = inputs.shape[2]
    parts = own_count // beams
    requests = beams // BEAM
    own_requests = own_count // BEAM
    heads = dense_weight.shape[0] // HD
    rank = lax.axis_index("req")
    assert parts == 2 and lax.axis_size("mlp") == 2 * ranks

    own_lengths = lax.dynamic_slice_in_dim(lengths, rank * own_requests, own_requests, 0)
    positions = jnp.broadcast_to(
        own_lengths.reshape(parts, 1, requests, 1)
        + jnp.arange(STEPS, dtype=jnp.int32).reshape(1, STEPS, 1, 1),
        (parts, STEPS, requests, BEAM),
    ).reshape(-1)
    tables = rotary_tables(positions)
    parent_wide = jnp.broadcast_to(parents[0][:, None], (own_count, LANES))

    with jax.named_scope("inputs_gather"):
        pieces = gather_pieces(inputs.reshape(STEPS * beams, width))
    with jax.named_scope("weight_sums"):
        weights = (attn_weight, up_weight, next_weight)
        sums = jnp.concatenate([weight_sums(norm_gains[k], w) for k, w in enumerate(weights)])
        sums = [part.reshape(-1) for part in exchange(sums.reshape(-1, LANES))]
        cuts = (0, weights[0].shape[1], weights[0].shape[1] + weights[1].shape[1], sums[0].shape[0])
        sums = [[part[a:b] for part in sums] for a, b in zip(cuts, cuts[1:])]
    with jax.named_scope("qkv"):
        partial, stats, *mlp_in = project(pieces, norm_gains[:2], attn_weight, STEPS)
        mixed = lax.psum_scatter(partial, "req", scatter_dimension=0, tiled=True)
    with jax.named_scope("statistics"):
        away, scale = own_statistics(stats, width, STEPS * beams)
    with jax.named_scope("up"):
        hiddens = []
        for s in range(STEPS):
            partial = jnp.dot(mlp_in[s], up_weight, preferred_element_type=F32).astype(BF16)
            partial, away, scale, sums = lax.optimization_barrier((partial, away, scale, sums))
            hiddens.append(lax.psum_scatter(partial, "req", scatter_dimension=0, tiled=True))

    def activate(s, hidden):
        at = slice(s * beams, (s + 1) * beams)
        with jax.named_scope("gelu"):
            hidden = corrected(hidden.astype(F32), away[..., at], scale[:, at], sums[1])
            own = jax.nn.gelu(hidden, approximate=False).astype(BF16)
        with jax.named_scope("activated_gather"):
            return (own,) + line_gather(own)

    with jax.named_scope("attention"):
        queries, keys, values = head_split(
            mixed, away, scale, sums[0], tables, heads, parts, requests
        )
        queries_all = exchange(queries)
        pieces = page_attention(
            queries_all, cache_keys, cache_values, slot_table, lengths, heads, ranks
        )
    hiddens[0], pieces = lax.optimization_barrier((hiddens[0], pieces))
    activated = [activate(0, hiddens[0])]
    with jax.named_scope("attention"):
        pieces = [pieces[0]] + [rotated(pieces[d], "req", d) for d in range(1, ranks)]
        attended = merge(queries, keys, values, parent_wide, pieces, heads, own_requests)
        attended = exchange(attended)
    hiddens[1], first = lax.optimization_barrier((hiddens[1], activated[0][1][0]))
    activated[0][1][0] = first
    activated.append(activate(1, hiddens[1]))
    layers, followings = [], []
    for s in range(STEPS):
        with jax.named_scope(f"down_{s}"):
            mine, other = layer_update(s, attended, *activated[s], dense_weight, down_weight)
            layer = (inputs[s].astype(F32) + scatter_sum(mine, other)).astype(BF16)
            if s + 1 < STEPS:
                activated[s + 1], layer = lax.optimization_barrier((activated[s + 1], layer))
            layers.append(layer)
        with jax.named_scope(f"next_{s}"):
            partial, stats = project(gather_pieces(layer), norm_gains[2:], next_weight, 1)
            total = lax.psum_scatter(partial, "req", scatter_dimension=0, tiled=True).astype(F32)
            away, scale = own_statistics(stats, width, beams)
            followings.append(corrected(total, away, scale, sums[2]).astype(BF16))
    return jnp.stack(layers), jnp.stack(followings)


def solution(mesh):
    in_specs = (
        P(None, "mlp", "req"),
        P(None, "req"),
        P("req", "mlp"),
        P("req", "mlp"),
        P("mlp", "req"),
        P("mlp", "req"),
        P("req", "mlp"),
        P("req", None, "mlp"),
        P("req", None, "mlp"),
        P(),
        P(None, "req"),
        P(None, "req"),
    )
    out_specs = (P(None, "mlp", "req"), P(None, "req", "mlp"))
    return jax.shard_map(shards, mesh=mesh, in_specs=in_specs, out_specs=out_specs, check_vma=False)
```

```python
import functools
import math

import jax
import jax.numpy as jnp
from jax import lax
from jax.experimental import pallas as pl
from jax.experimental.pallas import tpu as pltpu
from jax.sharding import PartitionSpec as P

HD = 128
ROT = 32
PAGE = 128
BEAM = 8
STEPS = 2
LANES = 128
STAT_ROWS = 16
GROUP = 8

NEG_FILL = -1e30
EPSILON = 1e-05
F32 = jnp.float32
BF16 = jnp.bfloat16


def rotated(array, axis, distance):
    size = lax.axis_size(axis)
    return lax.ppermute(array, axis, [(k, (k + distance) % size) for k in range(size)])


def flipped(array, axis, bits):
    return lax.ppermute(array, axis, [(k, k ^ bits) for k in range(lax.axis_size(axis))])


def gather_pieces(block):
    pairs = lax.axis_size("mlp") // 2
    near = [block] + [flipped(block, "mlp", 2 * d) for d in range(1, pairs)]
    far = [flipped(piece, "mlp", 1) for piece in near]
    return near + far


def scatter_sum(mine, other):
    size = lax.axis_size("req")
    pair = lax.axis_index("mlp") // 2
    summed = (mine.astype(F32) + flipped(other, "mlp", 1).astype(F32)).astype(BF16)

    def block(owner):
        return lax.dynamic_index_in_dim(summed, owner, 0, keepdims=False)

    total = block(pair).astype(F32)
    for d in range(1, size):
        total = total + flipped(block(pair ^ d), "mlp", 2 * d).astype(F32)
    return total


def after(value, *others):
    return lax.optimization_barrier((value,) + others)[0]


def eye_mask(rows):
    shape = (rows, LANES)
    return lax.broadcasted_iota(jnp.int32, shape, 0) == lax.broadcasted_iota(jnp.int32, shape, 1)


def project_kernel(count, widths, place_ref, gain_ref, weight_ref, *refs):
    pieces, refs = refs[:count], refs[count:]
    outs, (stats, *extra, held) = refs[: len(widths)], refs[len(widths) :]
    rows = pieces[0].shape[0]

    @pl.when(pl.program_id(0) == 0)
    def _():
        eye = eye_mask(rows)
        pair, core = place_ref[0] // 2, place_ref[0] % 2
        for k in range(count):
            d, away = k % (count // 2), k // (count // 2)
            owner = (pair ^ d) * 2 + (core ^ away)
            value = pieces[k][...].astype(F32)
            mean = jnp.mean(value, axis=1, keepdims=True)
            centred = value - mean
            square = jnp.sum(centred * centred, axis=1, keepdims=True)
            for row, column in ((owner, mean), (count + owner, square)):
                stats[pl.ds(row, 1), :] = jnp.sum(
                    jnp.where(eye, column, 0.0), axis=0, keepdims=True
                )
            at = pl.ds(pl.multiple_of(owner * rows, rows), rows)
            held[at, :] = (centred * gain_ref[0:1, :]).astype(BF16)
            if extra:
                extra[0][at, :] = (centred * gain_ref[1:2, :]).astype(BF16)

    result = jnp.dot(held[...], weight_ref[...], preferred_element_type=F32).astype(BF16)
    for k, out in enumerate(outs):
        out[...] = result[:, sum(widths[:k]) : sum(widths[: k + 1])]


def project(pieces, gains, weight, widths):
    count = len(pieces)
    rows, width = pieces[0].shape
    columns = weight.shape[1]
    tile = sum(widths)
    steps = columns // tile
    place = lax.axis_index("mlp").astype(jnp.int32).reshape(1)
    extra = jax.ShapeDtypeStruct((count * rows, width), BF16)
    extras = (extra,) * (gains.shape[0] - 1)
    stats = jax.ShapeDtypeStruct((2 * count, LANES), F32)
    return pl.pallas_call(
        functools.partial(project_kernel, count, widths),
        out_shape=tuple(jax.ShapeDtypeStruct((count * rows, steps * w), BF16) for w in widths)
        + (stats,)
        + extras,
        grid=(steps,),
        in_specs=[
            pl.BlockSpec(memory_space=pltpu.SMEM),
            full_block(gains.shape),
            pl.BlockSpec((width, tile), lambda n: (0, n)),
        ]
        + [full_block((rows, width))] * count,
        out_specs=[pl.BlockSpec((count * rows, w), lambda n: (0, n)) for w in widths]
        + [full_block(stats.shape)]
        + [full_block(extra.shape)] * len(extras),
        scratch_shapes=[pltpu.VMEM((count * rows, width), BF16)],
        compiler_params=pltpu.CompilerParams(vmem_limit_bytes=32 << 20),
        cost_estimate=pl.CostEstimate(
            flops=2 * count * rows * width * columns,
            bytes_accessed=2 * (width * columns + count * rows * (2 * width + columns)),
            transcendentals=0,
        ),
    )(place, gains, in_hbm(weight), *pieces)


def next_kernel(count, ranks, place_ref, gain_ref, weight_ref, *refs):
    pieces, (out, held) = refs[:count], refs[count:]
    rows = pieces[0].shape[0]
    tile = weight_ref.shape[1]
    step = pl.program_id(0)

    @pl.when(step == 0)
    def _():
        lane = lax.broadcasted_iota(jnp.int32, (rows, LANES), 1)
        pair, core, rank = place_ref[0] // 2, place_ref[0] % 2, place_ref[1]
        for k in range(count):
            d, away = k % (count // 2), k // (count // 2)
            owner = (pair ^ d) * 2 + (core ^ away)
            value = pieces[k][...].astype(F32)
            mean = jnp.mean(value, axis=1, keepdims=True)
            centred = value - mean
            square = jnp.sum(centred * centred, axis=1, keepdims=True)
            columns = jnp.zeros((rows, LANES), F32)
            for j, rest in enumerate((mean, square)):
                for part in range(3):
                    rounded = rest.astype(BF16).astype(F32)
                    rest = rest - rounded
                    at = (j * 3 + part) * ranks + rank
                    columns = jnp.where(lane == at, rounded, columns)
            at = pl.ds(pl.multiple_of(owner * rows, rows), rows)
            held[at, :] = (centred * gain_ref[...]).astype(BF16)
            out[at, out.shape[1] - LANES :] = columns.astype(BF16)

    result = jnp.dot(held[...], weight_ref[...], preferred_element_type=F32)
    out[:, pl.ds(pl.multiple_of(step * tile, tile), tile)] = result.astype(BF16)


def project_next(pieces, gain, weight):
    count = len(pieces)
    rows, width = pieces[0].shape
    columns = weight.shape[1]
    ranks = lax.axis_size("req")
    tile = math.gcd(columns, 256)
    place = jnp.stack([lax.axis_index("mlp"), lax.axis_index("req")]).astype(jnp.int32)
    out = jax.ShapeDtypeStruct((count * rows, columns + LANES), BF16)
    return pl.pallas_call(
        functools.partial(next_kernel, count, ranks),
        out_shape=out,
        grid=(columns // tile,),
        in_specs=[
            pl.BlockSpec(memory_space=pltpu.SMEM),
            full_block(gain.shape),
            pl.BlockSpec((width, tile), lambda n: (0, n)),
        ]
        + [full_block((rows, width))] * count,
        out_specs=full_block(out.shape),
        scratch_shapes=[pltpu.VMEM((count * rows, width), BF16)],
        compiler_params=pltpu.CompilerParams(vmem_limit_bytes=32 << 20),
        cost_estimate=pl.CostEstimate(
            flops=2 * count * rows * width * columns,
            bytes_accessed=2 * (width * columns + count * rows * (width + columns)),
            transcendentals=0,
        ),
    )(place, gain, in_hbm(weight), *pieces)


def exchange(part):
    return [part] + [rotated(part, "req", d) for d in range(1, lax.axis_size("req"))]


def own_statistics(stats, width, rows):
    size = lax.axis_size("req")
    count = stats.shape[0] // 2
    parts = jnp.stack(exchange(stats)).reshape(size, 2, count, LANES)
    parts = lax.dynamic_slice_in_dim(parts, 2 * lax.axis_index("req"), 2, 2)[..., :rows]
    mean = jnp.mean(parts[:, 0], axis=0)
    away = parts[:, 0] - mean
    square = jnp.sum(parts[:, 1] + width * jnp.square(away), axis=0)
    return away, lax.rsqrt(square / (width * size) + EPSILON)


def weight_sums(gain, weight):
    high = gain.astype(BF16)
    low = (gain - high.astype(F32)).astype(BF16)
    rows = jnp.concatenate([high[None], low[None], jnp.zeros((14, gain.shape[0]), BF16)])
    both = jnp.dot(rows, weight, preferred_element_type=F32)
    return both[0:1] + both[1:2]


def stat_columns(away, scale):
    ranks = away.shape[0]
    stats = jnp.concatenate([away.reshape(ranks, -1), scale.reshape(1, -1)]).T
    return jnp.pad(stats, ((0, 0), (0, LANES - ranks - 1)))


def corrected(total, stat_ref, sums):
    ranks = sums.shape[0]
    for d in range(ranks):
        total = total + stat_ref[:, d : d + 1] * sums[d : d + 1, :]
    return total * stat_ref[:, ranks : ranks + 1]


def activate_kernel(beams, total_ref, stat_ref, sum_ref, *outs):
    total = corrected(total_ref[...].astype(F32), stat_ref, sum_ref[...])
    total = (0.5 * total * (1.0 + lax.erf(total * math.sqrt(0.5)))).astype(BF16)
    for part in range(total.shape[0] // (STEPS * beams)):
        for s in range(STEPS):
            first = (part * STEPS + s) * beams
            outs[s][part * beams : (part + 1) * beams, :] = total[first : first + beams]


def activate(total, stats, sums, first, beams):
    rows, columns = total.shape
    tile = math.gcd(math.gcd(columns, 512), first)
    out = pl.BlockSpec((rows // STEPS, tile), lambda n: (0, n))
    return pl.pallas_call(
        functools.partial(activate_kernel, beams),
        out_shape=(jax.ShapeDtypeStruct((rows // STEPS, columns), BF16),) * STEPS,
        grid=(columns // tile,),
        in_specs=[
            pl.BlockSpec((rows, tile), lambda n: (0, n)),
            full_block(stats.shape),
            pl.BlockSpec((sums.shape[0], tile), lambda n: (0, first // tile + n)),
        ],
        out_specs=(out,) * STEPS,
        compiler_params=pltpu.CompilerParams(vmem_limit_bytes=24 << 20),
    )(total, stats, sums)


def finish_kernel(ranks, width, rank_ref, *refs):
    totals, columns, (sum_ref, out) = refs[:STEPS], refs[STEPS : 2 * STEPS], refs[2 * STEPS :]
    for s in range(STEPS):
        held = columns[s][...].astype(F32)
        lane = lax.broadcasted_iota(jnp.int32, held.shape, 1)

        def column(j, d):
            at = j * 3 * ranks + lax.rem(rank_ref[0] + ranks - d, ranks)
            chosen = (lane == at) | (lane == at + ranks) | (lane == at + 2 * ranks)
            return jnp.sum(jnp.where(chosen, held, 0.0), axis=1, keepdims=True)

        means = [column(0, d) for d in range(ranks)]
        mean = sum(means[1:], means[0]) * (1.0 / ranks)
        square = jnp.zeros_like(mean)
        total = totals[s][...].astype(F32)
        for d in range(ranks):
            away = means[d] - mean
            square = square + column(1, d) + width * away * away
            total = total + away * sum_ref[d : d + 1, :]
        out[s] = (total * lax.rsqrt(square * (1.0 / (width * ranks)) + EPSILON)).astype(BF16)


def finish(totals, sums, first, width):
    rows = totals[0].shape[0]
    columns = totals[0].shape[1] - LANES
    tile = math.gcd(math.gcd(columns, 512), first)
    ranks = lax.axis_size("req")
    rank = lax.axis_index("req").astype(jnp.int32).reshape(1)
    totals = [in_hbm(total) for total in totals]
    return pl.pallas_call(
        functools.partial(finish_kernel, ranks, width),
        out_shape=jax.ShapeDtypeStruct((STEPS, rows, columns), BF16),
        grid=(columns // tile,),
        in_specs=[pl.BlockSpec(memory_space=pltpu.SMEM)]
        + [pl.BlockSpec((rows, tile), lambda n: (0, n))] * STEPS
        + [pl.BlockSpec((rows, LANES), lambda n: (0, columns // LANES))] * STEPS
        + [pl.BlockSpec((sums.shape[0], tile), lambda n: (0, first // tile + n))],
        out_specs=pl.BlockSpec((STEPS, rows, tile), lambda n: (0, 0, n)),
        compiler_params=pltpu.CompilerParams(vmem_limit_bytes=24 << 20),
    )(rank, *totals, *totals, sums)


def update_kernel(ranks, step, place_ref, hidden_ref, down_ref, dense_ref, *refs):
    attended, (mine, other, heads) = refs[:ranks], refs[ranks:]
    rows = hidden_ref.shape[0] // ranks
    rank, core = place_ref[0], place_ref[1]

    @pl.when(pl.program_id(0) == 0)
    def _():
        for d in range(ranks):
            owner = lax.rem(rank + ranks - d, ranks)
            heads[pl.ds(pl.multiple_of(owner * rows, rows), rows), :] = attended[d][
                step * rows : (step + 1) * rows, :
            ]

    result = jnp.dot(hidden_ref[...], down_ref[...], preferred_element_type=F32) + jnp.dot(
        heads[...], dense_ref[...], preferred_element_type=F32
    )
    half = rows // 2
    for k in range(ranks):
        first = result[k * rows : k * rows + half]
        second = result[k * rows + half : (k + 1) * rows]
        mine[k] = jnp.where(core == 0, first, second).astype(BF16)
        other[k] = jnp.where(core == 0, second, first).astype(BF16)


def layer_update(step, hidden, attended, dense_weight, down_weight):
    ranks = lax.axis_size("req")
    rows, columns = hidden.shape
    head_width, width = dense_weight.shape
    tile = min(256, width)
    place = jnp.stack([lax.axis_index("req"), lax.axis_index("mlp") % 2]).astype(jnp.int32)
    shape = jax.ShapeDtypeStruct((ranks, rows // ranks // 2, width), BF16)
    out_block = pl.BlockSpec((ranks, rows // ranks // 2, tile), lambda n: (0, 0, n))
    return pl.pallas_call(
        functools.partial(update_kernel, ranks, step),
        out_shape=(shape, shape),
        grid=(width // tile,),
        in_specs=[
            pl.BlockSpec(memory_space=pltpu.SMEM),
            full_block(hidden.shape),
            pl.BlockSpec((columns, tile), lambda n: (0, n)),
            pl.BlockSpec((head_width, tile), lambda n: (0, n)),
        ]
        + [full_block(attended[0].shape)] * ranks,
        out_specs=(out_block, out_block),
        scratch_shapes=[pltpu.VMEM((rows, head_width), BF16)],
        compiler_params=pltpu.CompilerParams(vmem_limit_bytes=40 << 20),
        cost_estimate=pl.CostEstimate(
            flops=2 * rows * (columns + head_width) * width,
            bytes_accessed=2 * (columns + head_width) * (width + rows),
            transcendentals=0,
        ),
    )(place, in_hbm(hidden), in_hbm(down_weight), in_hbm(dense_weight), *attended)


def rotary_tables(positions):
    lane = jnp.arange(HD, dtype=jnp.int32)[None, :]
    half = ROT // 2
    freq = jnp.exp((lane % half).astype(F32) * (-2.0 * math.log(10000.0) / ROT))
    angles = positions.astype(F32)[:, None] * freq
    cosine = jnp.where(lane < ROT, jnp.cos(angles), 1.0)
    sine = jnp.sin(angles)
    upper = jnp.where(lane < half, -sine, 0.0)
    lower = jnp.where((lane >= half) & (lane < ROT), sine, 0.0)
    return cosine, upper, lower


def in_hbm(array):
    return pltpu.with_memory_space_constraint(array, pltpu.HBM)


def full_block(shape):
    return pl.BlockSpec(shape, lambda *_: (0,) * len(shape))


def turn(value, tables):
    return (
        value * tables[0][...]
        + pltpu.roll(value, HD - ROT // 2, 1) * tables[1][...]
        + pltpu.roll(value, ROT // 2, 1) * tables[2][...]
    )


def store_head(out, value, head, heads, parts, requests):
    rows = requests * BEAM
    for part in range(parts):
        for request in range(requests):
            first = part * STEPS * rows + request * BEAM
            pair = [value[first + s * rows : first + s * rows + BEAM] for s in range(STEPS)]
            at = ((part * requests + request) * heads + head) * STEPS * BEAM
            out[at : at + STEPS * BEAM, :] = jnp.concatenate(pair, axis=0).astype(BF16)


def query_kernel(heads, parts, requests, rank_ref, own_ref, *refs):
    received, (stat_ref, sum_ref, *tables, out) = refs[:-6], refs[-6:]
    for head in range(heads):
        at = slice(head * HD, (head + 1) * HD)
        value = own_ref[0, :, at].astype(F32)
        for piece in received:
            value = value + piece[:, at].astype(F32)
        first = head * 3 * HD
        value = corrected(value, stat_ref, sum_ref[:, first : first + HD])
        store_head(out, turn(value, tables), head, heads, parts, requests)


def split_queries(partial, received, stats, sums, tables, heads, parts, requests):
    rank = lax.axis_index("req").astype(jnp.int32).reshape(1)
    operands = (*received, stats, sums, *tables)
    rows = parts * requests * heads * STEPS * BEAM
    return pl.pallas_call(
        functools.partial(query_kernel, heads, parts, requests),
        out_shape=jax.ShapeDtypeStruct((rows, HD), BF16),
        grid_spec=pltpu.PrefetchScalarGridSpec(
            num_scalar_prefetch=1,
            grid=(1,),
            in_specs=[pl.BlockSpec((1,) + partial.shape[1:], lambda n, r: (r[0], 0, 0))]
            + [full_block(operand.shape) for operand in operands],
            out_specs=full_block((rows, HD)),
        ),
        compiler_params=pltpu.CompilerParams(vmem_limit_bytes=24 << 20),
    )(rank, partial, *operands)


def key_value_kernel(heads, parts, requests, x_ref, stat_ref, sum_ref, *refs):
    tables, outs = refs[:3], refs[3:]
    for head in range(heads):
        for kind, out in enumerate(outs):
            column = (head * 2 + kind) * HD
            value = x_ref[:, column : column + HD].astype(F32)
            column = (head * 3 + kind + 1) * HD
            value = corrected(value, stat_ref, sum_ref[:, column : column + HD])
            if kind == 0:
                value = turn(value, tables)
            store_head(out, value, head, heads, parts, requests)


def split_keys_values(total, stats, sums, tables, heads, parts, requests):
    shape = jax.ShapeDtypeStruct((parts * requests * heads * STEPS * BEAM, HD), BF16)
    return pl.pallas_call(
        functools.partial(key_value_kernel, heads, parts, requests),
        out_shape=(shape, shape),
        compiler_params=pltpu.CompilerParams(vmem_limit_bytes=24 << 20),
    )(total, stats, sums, *tables)


def page_kernel(heads, ranks, own_rows, slot_ref, length_ref, me_ref, k_ref, v_ref, *rest):
    queries, outs = rest[:ranks], rest[ranks : 2 * ranks]
    q_ref, top_ref, sum_ref, out_ref = rest[2 * ranks :]
    step = pl.program_id(0)
    height = heads * STEPS * BEAM
    chunk = STEPS * BEAM
    scale = 1.0 / math.sqrt(HD)

    @pl.when(step == 0)
    def _():
        for d in range(ranks):
            rank = lax.rem(me_ref[0] + ranks - d, ranks)
            q_ref[pl.ds(pl.multiple_of(rank * own_rows, own_rows), own_rows), :] = queries[d][...]
        top_ref[...] = jnp.full(top_ref.shape, NEG_FILL, F32)
        sum_ref[...] = jnp.zeros(sum_ref.shape, F32)
        out_ref[...] = jnp.zeros(out_ref.shape, F32)

    lane = lax.broadcasted_iota(jnp.int32, (height, PAGE), 1)
    found = []
    for g in range(GROUP):
        slot = step * GROUP + g
        owner = slot_ref[0, slot]
        valid = jnp.maximum(owner, 0)
        limit = jnp.where(owner >= 0, length_ref[valid] - slot_ref[1, slot] * PAGE, 0)
        base = pl.multiple_of(valid * height, height)
        scores = []
        for h in range(heads):
            query = q_ref[pl.ds(pl.multiple_of(base + h * chunk, chunk), chunk), :]
            key = k_ref[g, :, h * HD : (h + 1) * HD]
            scores.append(
                lax.dot_general(query, key, (((1,), (1,)), ((), ())), preferred_element_type=F32)
            )
        live = lane < limit
        score = jnp.where(live, jnp.concatenate(scores, axis=0) * scale, NEG_FILL)
        top = jnp.max(score, axis=1, keepdims=True)
        weight = jnp.where(live, jnp.exp(score - top), 0.0)
        total = jnp.sum(weight, axis=1, keepdims=True)
        weight = weight.astype(BF16)
        value = [
            jnp.dot(
                weight[h * chunk : (h + 1) * chunk],
                v_ref[g, :, h * HD : (h + 1) * HD],
                preferred_element_type=F32,
            )
            for h in range(heads)
        ]
        found.append((base, top, total, jnp.concatenate(value, axis=0)))
    for base, top, total, value in found:
        at = pl.ds(base, height)
        old = top_ref[at, :]
        new = jnp.maximum(old, top)
        left = jnp.exp(old - new)
        right = jnp.exp(top - new)
        top_ref[at, :] = new
        sum_ref[at, :] = sum_ref[at, :] * left + total * right
        out_ref[at, :] = out_ref[at, :] * left + value * right

    @pl.when(step == pl.num_programs(0) - 1)
    def _():
        eye = lax.broadcasted_iota(jnp.int32, (LANES, LANES), 0) == lax.broadcasted_iota(
            jnp.int32, (LANES, LANES), 1
        )
        blocks = own_rows // LANES
        for d in range(ranks):
            rank = lax.rem(me_ref[0] + d, ranks)
            levels = []
            for block in range(blocks):
                first = pl.multiple_of(rank * own_rows + block * LANES, LANES)
                total = sum_ref[pl.ds(first, LANES), :]
                some = total > 0.0
                total = jnp.where(some, total, 1.0)
                outs[d][block * LANES : (block + 1) * LANES, :] = (
                    out_ref[pl.ds(first, LANES), :] / total
                ).astype(BF16)
                level = jnp.where(some, top_ref[pl.ds(first, LANES), :] + jnp.log(total), NEG_FILL)
                levels.append(jnp.sum(jnp.where(eye, level, 0.0), axis=0, keepdims=True))
            levels.append(jnp.zeros((STAT_ROWS - blocks, LANES), F32))
            level = jnp.concatenate(levels, axis=0)
            for k in range(3):
                rounded = level.astype(BF16)
                level = level - rounded.astype(F32)
                outs[d][own_rows + k * STAT_ROWS : own_rows + (k + 1) * STAT_ROWS, :] = rounded


def page_attention(queries, keys, values, slot_table, lengths, heads, ranks):
    slots = keys.shape[0]
    own_rows = queries[0].shape[0]
    rows = own_rows * ranks
    me = lax.axis_index("req").astype(jnp.int32).reshape(1)
    out_rows = own_rows + 3 * STAT_ROWS
    shape = jax.ShapeDtypeStruct((out_rows, LANES), BF16)
    page_block = pl.BlockSpec((GROUP, PAGE, heads * HD), lambda g, *_: (g, 0, 0))
    return pl.pallas_call(
        functools.partial(page_kernel, heads, ranks, own_rows),
        out_shape=(shape,) * ranks,
        grid_spec=pltpu.PrefetchScalarGridSpec(
            num_scalar_prefetch=3,
            grid=(slots // GROUP,),
            in_specs=[page_block, page_block] + [full_block((own_rows, HD))] * ranks,
            out_specs=[full_block((out_rows, LANES))] * ranks,
            scratch_shapes=[pltpu.VMEM((rows, HD), BF16)] + [pltpu.VMEM((rows, LANES), F32)] * 3,
        ),
        compiler_params=pltpu.CompilerParams(vmem_limit_bytes=40 << 20),
        cost_estimate=pl.CostEstimate(
            flops=4 * slots * PAGE * heads * HD * STEPS * BEAM,
            bytes_accessed=8 * slots * PAGE * heads * HD * 2,
            transcendentals=slots * PAGE * heads * STEPS * BEAM,
        ),
    )(slot_table, lengths, me, in_hbm(keys), in_hbm(values), *queries)


def merge_kernel(heads, ranks, parts, requests, q_ref, k_ref, v_ref, parent_ref, *rest):
    pieces, out, work = rest[:ranks], rest[ranks], rest[ranks + 1]
    chunk = STEPS * BEAM
    height = heads * chunk
    own_rows = q_ref.shape[0]
    scale = 1.0 / math.sqrt(HD)
    eye = lax.broadcasted_iota(jnp.int32, (LANES, LANES), 0) == lax.broadcasted_iota(
        jnp.int32, (LANES, LANES), 1
    )
    late = lax.broadcasted_iota(jnp.int32, (LANES, 1), 0) % chunk >= BEAM
    levels = []
    for piece in pieces:
        level = jnp.zeros((STAT_ROWS, LANES), F32)
        for k in range(3):
            first = own_rows + k * STAT_ROWS
            level = level + piece[first : first + STAT_ROWS, :].astype(F32)
        levels.append(level)
    for block in range(own_rows // LANES):
        at = slice(block * LANES, (block + 1) * LANES)
        query = q_ref[at, :].astype(F32)
        key = k_ref[at, :].astype(F32)
        value = v_ref[at, :].astype(F32)
        held_keys, held_values = [], []
        for tile in range(LANES // chunk):
            first = tile * chunk
            request = (block * LANES + first) // height
            parent = parent_ref[request * BEAM : (request + 1) * BEAM, :]
            for held, source in ((held_keys, key), (held_values, value)):
                chosen = jnp.zeros((BEAM, HD), F32)
                for beam in range(BEAM):
                    row = source[first + beam : first + beam + 1, :]
                    chosen = jnp.where(parent == beam, row, chosen)
                held += [jnp.zeros((BEAM, HD), F32), chosen]
        held_key = jnp.concatenate(held_keys, axis=0)
        held_value = jnp.concatenate(held_values, axis=0)
        own = jnp.sum(query * key, axis=1, keepdims=True) * scale
        past = jnp.sum(query * held_key, axis=1, keepdims=True) * scale
        past = jnp.where(late, past, NEG_FILL)
        columns = [
            jnp.sum(jnp.where(eye, level[block : block + 1, :], 0.0), axis=1, keepdims=True)
            for level in levels
        ]
        top = functools.reduce(jnp.maximum, columns, jnp.maximum(own, past))
        own = jnp.exp(own - top)
        past = jnp.where(late, jnp.exp(past - top), 0.0)
        total = own + past
        result = own * value + past * held_value
        for column, piece in zip(columns, pieces):
            factor = jnp.exp(column - top)
            total = total + factor
            result = result + factor * piece[at, :].astype(F32)
        work[at, :] = result / total
    rows = requests * BEAM
    for part in range(parts):
        for request in range(0, requests, 2):
            for head in range(heads):
                for s in range(STEPS):
                    tiles = []
                    for r in (request, request + 1):
                        first = (part * requests + r) * height + head * chunk + s * BEAM
                        tiles.append(work[first : first + BEAM, :])
                    first = (s * parts + part) * rows + request * BEAM
                    out[first : first + 2 * BEAM, head * HD : (head + 1) * HD] = jnp.concatenate(
                        tiles, axis=0
                    ).astype(BF16)


def merge(queries, keys, values, parents, pieces, heads, parts, requests):
    ranks = len(pieces)
    rows = STEPS * parts * requests * BEAM
    return pl.pallas_call(
        functools.partial(merge_kernel, heads, ranks, parts, requests),
        out_shape=jax.ShapeDtypeStruct((rows, heads * HD), BF16),
        scratch_shapes=[pltpu.VMEM(queries.shape, F32)],
        compiler_params=pltpu.CompilerParams(vmem_limit_bytes=32 << 20),
    )(queries, keys, values, parents, *pieces)


def shards(
    inputs,
    norm_gains,
    attn_weight,
    up_weight,
    dense_weight,
    down_weight,
    next_weight,
    cache_keys,
    cache_values,
    lengths,
    slot_table,
    parents,
):
    ranks = lax.axis_size("req")
    own_count = parents.shape[1]
    beams = inputs.shape[1]
    width = inputs.shape[2]
    parts = own_count // beams
    requests = beams // BEAM
    own_requests = own_count // BEAM
    heads = dense_weight.shape[0] // HD
    rank = lax.axis_index("req")
    assert parts == 2 and lax.axis_size("mlp") == 2 * ranks

    own_lengths = lax.dynamic_slice_in_dim(lengths, rank * own_requests, own_requests, 0)
    positions = jnp.broadcast_to(
        own_lengths.reshape(parts, 1, requests, 1)
        + jnp.arange(STEPS, dtype=jnp.int32).reshape(1, STEPS, 1, 1),
        (parts, STEPS, requests, BEAM),
    ).reshape(-1)
    tables = rotary_tables(positions)
    parent_wide = jnp.broadcast_to(parents[0][:, None], (own_count, LANES))

    with jax.named_scope("inputs_gather"):
        pieces = gather_pieces(inputs.reshape(STEPS * beams, width))
    with jax.named_scope("qkv"):
        query, key_value, stats, mlp_in = project(
            pieces, norm_gains[:2], attn_weight, (HD, 2 * HD)
        )
        key_value = lax.psum_scatter(key_value, "req", scatter_dimension=0, tiled=True)
        query = query.reshape(ranks, -1, query.shape[1])
        received = [
            rotated(
                lax.dynamic_index_in_dim(query, (rank + d) % ranks, 0, keepdims=False), "req", d
            )
            for d in range(1, ranks)
        ]
    with jax.named_scope("weight_sums"):
        weights = (attn_weight, up_weight, next_weight)
        sums = [weight_sums(norm_gains[k], w) for k, w in enumerate(weights)]
        sums = jnp.concatenate(exchange(jnp.concatenate(sums, axis=1)))
        up_first = attn_weight.shape[1]
        next_first = up_first + up_weight.shape[1]
    with jax.named_scope("statistics"):
        stats = stat_columns(*own_statistics(stats, width, STEPS * beams))
    with jax.named_scope("queries"):
        queries = split_queries(query, received, stats, sums, tables, heads, parts, requests)
        queries_all = exchange(queries)
    with jax.named_scope("up"):
        up = jnp.dot(after(mlp_in, queries), up_weight, preferred_element_type=F32).astype(BF16)
        up = lax.psum_scatter(up, "req", scatter_dimension=0, tiled=True)
    with jax.named_scope("pages"):
        pieces = page_attention(
            queries_all, cache_keys, cache_values, slot_table, lengths, heads, ranks
        )
        pieces = [pieces[0]] + [rotated(pieces[d], "req", d) for d in range(1, ranks)]
    with jax.named_scope("merge"):
        key_value = after(key_value, pieces[0])
        keys, values = split_keys_values(
            key_value, stats, sums, tables, heads, parts, requests
        )
        attended = merge(queries, keys, values, parent_wide, pieces, heads, parts, requests)
        attended_all = exchange(attended)
    with jax.named_scope("activated"):
        activated = activate(after(up, attended), stats, sums, up_first, beams)
        activated = [lax.all_gather(own, "req", axis=0, tiled=True) for own in activated]
    layers, totals = [], []
    for s in range(STEPS):
        with jax.named_scope(f"down_{s}"):
            mine, other = layer_update(s, activated[s], attended_all, dense_weight, down_weight)
            layer = (inputs[s].astype(F32) + scatter_sum(mine, other)).astype(BF16)
            layers.append(layer)
        with jax.named_scope(f"next_{s}"):
            partial = project_next(gather_pieces(layer), norm_gains[2:], next_weight)
            if s + 1 < STEPS:
                activated[s + 1] = after(activated[s + 1], partial)
            totals.append(lax.psum_scatter(partial, "req", scatter_dimension=0, tiled=True))
    return jnp.stack(layers), finish(totals, sums, next_first, width)


def solution(mesh):
    in_specs = (
        P(None, "mlp", "req"),
        P(None, "req"),
        P("req", "mlp"),
        P("req", "mlp"),
        P("mlp", "req"),
        P("mlp", "req"),
        P("req", "mlp"),
        P("req", None, "mlp"),
        P("req", None, "mlp"),
        P(),
        P(None, "req"),
        P(None, "req"),
    )
    out_specs = (P(None, "mlp", "req"), P(None, "req", "mlp"))
    return jax.shard_map(shards, mesh=mesh, in_specs=in_specs, out_specs=out_specs, check_vma=False)
```

```python
import functools
import math

import jax
import jax.numpy as jnp
from jax import lax
from jax.experimental import pallas as pl
from jax.experimental.pallas import tpu as pltpu
from jax.sharding import PartitionSpec as P

HD = 128
ROT = 32
PAGE = 128
BEAM = 8
STEPS = 2
LANES = 128
STAT_ROWS = 16
GROUP = 8

NEG_FILL = -1e30
EPSILON = 1e-05
F32 = jnp.float32
BF16 = jnp.bfloat16


def rotated(array, axis, distance):
    size = lax.axis_size(axis)
    return lax.ppermute(array, axis, [(k, (k + distance) % size) for k in range(size)])


def flipped(array, axis, bits):
    return lax.ppermute(array, axis, [(k, k ^ bits) for k in range(lax.axis_size(axis))])


def gather_pieces(block):
    pairs = lax.axis_size("mlp") // 2
    near = [block] + [flipped(block, "mlp", 2 * d) for d in range(1, pairs)]
    far = [flipped(piece, "mlp", 1) for piece in near]
    return near + far


def scatter_sum(mine, other):
    size = lax.axis_size("req")
    pair = lax.axis_index("mlp") // 2
    summed = (mine.astype(F32) + flipped(other, "mlp", 1).astype(F32)).astype(BF16)

    def block(owner):
        return lax.dynamic_index_in_dim(summed, owner, 0, keepdims=False)

    total = block(pair).astype(F32)
    for d in range(1, size):
        total = total + flipped(block(pair ^ d), "mlp", 2 * d).astype(F32)
    return total


def after(value, *others):
    return lax.optimization_barrier((value,) + others)[0]


def line_gather(block):
    size = lax.axis_size("req")
    rights, lefts = [], []
    right = left = block
    for t in range(1, size):
        right = lax.ppermute(right, "req", [(k, k + 1) for k in range(t - 1, size - 1)])
        left = lax.ppermute(left, "req", [(k + 1, k) for k in range(size - t)])
        rights.append(right)
        lefts.append(left)
    return rights, lefts


def eye_mask(rows):
    shape = (rows, LANES)
    return lax.broadcasted_iota(jnp.int32, shape, 0) == lax.broadcasted_iota(jnp.int32, shape, 1)


def project_kernel(count, widths, place_ref, gain_ref, weight_ref, *refs):
    pieces, refs = refs[:count], refs[count:]
    outs, (stats, *extra, held) = refs[: len(widths)], refs[len(widths) :]
    rows = pieces[0].shape[0]

    @pl.when(pl.program_id(0) == 0)
    def _():
        eye = eye_mask(rows)
        pair, core = place_ref[0] // 2, place_ref[0] % 2
        for k in range(count):
            d, away = k % (count // 2), k // (count // 2)
            owner = (pair ^ d) * 2 + (core ^ away)
            value = pieces[k][...].astype(F32)
            mean = jnp.mean(value, axis=1, keepdims=True)
            centred = value - mean
            square = jnp.sum(centred * centred, axis=1, keepdims=True)
            for row, column in ((owner, mean), (count + owner, square)):
                stats[pl.ds(row, 1), :] = jnp.sum(
                    jnp.where(eye, column, 0.0), axis=0, keepdims=True
                )
            at = pl.ds(pl.multiple_of(owner * rows, rows), rows)
            held[at, :] = (centred * gain_ref[0:1, :]).astype(BF16)
            if extra:
                extra[0][at, :] = (centred * gain_ref[1:2, :]).astype(BF16)

    result = jnp.dot(held[...], weight_ref[...], preferred_element_type=F32).astype(BF16)
    for k, out in enumerate(outs):
        out[...] = result[:, sum(widths[:k]) : sum(widths[: k + 1])]


def project(pieces, gains, weight, widths):
    count = len(pieces)
    rows, width = pieces[0].shape
    columns = weight.shape[1]
    tile = sum(widths)
    steps = columns // tile
    place = lax.axis_index("mlp").astype(jnp.int32).reshape(1)
    extra = jax.ShapeDtypeStruct((count * rows, width), BF16)
    extras = (extra,) * (gains.shape[0] - 1)
    stats = jax.ShapeDtypeStruct((2 * count, LANES), F32)
    return pl.pallas_call(
        functools.partial(project_kernel, count, widths),
        out_shape=tuple(jax.ShapeDtypeStruct((count * rows, steps * w), BF16) for w in widths)
        + (stats,)
        + extras,
        grid=(steps,),
        in_specs=[
            pl.BlockSpec(memory_space=pltpu.SMEM),
            full_block(gains.shape),
            pl.BlockSpec((width, tile), lambda n: (0, n)),
        ]
        + [full_block((rows, width))] * count,
        out_specs=[pl.BlockSpec((count * rows, w), lambda n: (0, n)) for w in widths]
        + [full_block(stats.shape)]
        + [full_block(extra.shape)] * len(extras),
        scratch_shapes=[pltpu.VMEM((count * rows, width), BF16)],
        compiler_params=pltpu.CompilerParams(vmem_limit_bytes=32 << 20),
        cost_estimate=pl.CostEstimate(
            flops=2 * count * rows * width * columns,
            bytes_accessed=2 * (width * columns + count * rows * (2 * width + columns)),
            transcendentals=0,
        ),
    )(place, gains, in_hbm(weight), *pieces)


def next_kernel(count, ranks, place_ref, gain_ref, weight_ref, *refs):
    pieces, (out, held) = refs[:count], refs[count:]
    rows = pieces[0].shape[0]
    tile = weight_ref.shape[1]
    step = pl.program_id(0)

    @pl.when(step == 0)
    def _():
        lane = lax.broadcasted_iota(jnp.int32, (rows, LANES), 1)
        pair, core, rank = place_ref[0] // 2, place_ref[0] % 2, place_ref[1]
        for k in range(count):
            d, away = k % (count // 2), k // (count // 2)
            owner = (pair ^ d) * 2 + (core ^ away)
            value = pieces[k][...].astype(F32)
            mean = jnp.mean(value, axis=1, keepdims=True)
            centred = value - mean
            square = jnp.sum(centred * centred, axis=1, keepdims=True)
            columns = jnp.zeros((rows, LANES), F32)
            for j, rest in enumerate((mean, square)):
                for part in range(3):
                    rounded = rest.astype(BF16).astype(F32)
                    rest = rest - rounded
                    at = (j * 3 + part) * ranks + rank
                    columns = jnp.where(lane == at, rounded, columns)
            at = pl.ds(pl.multiple_of(owner * rows, rows), rows)
            held[at, :] = (centred * gain_ref[...]).astype(BF16)
            out[at, out.shape[1] - LANES :] = columns.astype(BF16)

    result = jnp.dot(held[...], weight_ref[...], preferred_element_type=F32)
    out[:, pl.ds(pl.multiple_of(step * tile, tile), tile)] = result.astype(BF16)


def project_next(pieces, gain, weight):
    count = len(pieces)
    rows, width = pieces[0].shape
    columns = weight.shape[1]
    ranks = lax.axis_size("req")
    tile = math.gcd(columns, 512)
    place = jnp.stack([lax.axis_index("mlp"), lax.axis_index("req")]).astype(jnp.int32)
    out = jax.ShapeDtypeStruct((count * rows, columns + LANES), BF16)
    return pl.pallas_call(
        functools.partial(next_kernel, count, ranks),
        out_shape=out,
        grid=(columns // tile,),
        in_specs=[
            pl.BlockSpec(memory_space=pltpu.SMEM),
            full_block(gain.shape),
            pl.BlockSpec((width, tile), lambda n: (0, n)),
        ]
        + [full_block((rows, width))] * count,
        out_specs=full_block(out.shape),
        scratch_shapes=[pltpu.VMEM((count * rows, width), BF16)],
        compiler_params=pltpu.CompilerParams(vmem_limit_bytes=32 << 20),
        cost_estimate=pl.CostEstimate(
            flops=2 * count * rows * width * columns,
            bytes_accessed=2 * (width * columns + count * rows * (width + columns)),
            transcendentals=0,
        ),
    )(place, gain, in_hbm(weight), *pieces)


def exchange(part):
    return [part] + [rotated(part, "req", d) for d in range(1, lax.axis_size("req"))]


def own_statistics(stats, width, rows):
    size = lax.axis_size("req")
    count = stats.shape[0] // 2
    parts = jnp.stack(exchange(stats)).reshape(size, 2, count, LANES)
    parts = lax.dynamic_slice_in_dim(parts, 2 * lax.axis_index("req"), 2, 2)[..., :rows]
    mean = jnp.mean(parts[:, 0], axis=0)
    away = parts[:, 0] - mean
    square = jnp.sum(parts[:, 1] + width * jnp.square(away), axis=0)
    return away, lax.rsqrt(square / (width * size) + EPSILON)


def weight_sums(gain, weight):
    high = gain.astype(BF16)
    low = (gain - high.astype(F32)).astype(BF16)
    rows = jnp.concatenate([high[None], low[None], jnp.zeros((14, gain.shape[0]), BF16)])
    both = jnp.dot(rows, weight, preferred_element_type=F32)
    return both[0:1] + both[1:2]


def stat_columns(away, scale):
    ranks = away.shape[0]
    stats = jnp.concatenate([away.reshape(ranks, -1), scale.reshape(1, -1)]).T
    return jnp.pad(stats, ((0, 0), (0, LANES - ranks - 1)))


def corrected(total, stat_ref, sums):
    ranks = sums.shape[0]
    for d in range(ranks):
        total = total + stat_ref[:, d : d + 1] * sums[d : d + 1, :]
    return total * stat_ref[:, ranks : ranks + 1]


def activate_kernel(beams, total_ref, stat_ref, sum_ref, *outs):
    total = corrected(total_ref[...].astype(F32), stat_ref, sum_ref[...])
    total = (0.5 * total * (1.0 + lax.erf(total * math.sqrt(0.5)))).astype(BF16)
    for part in range(total.shape[0] // (STEPS * beams)):
        for s in range(STEPS):
            first = (part * STEPS + s) * beams
            outs[s][part * beams : (part + 1) * beams, :] = total[first : first + beams]


def activate(total, stats, sums, first, beams):
    rows, columns = total.shape
    tile = math.gcd(math.gcd(columns, 512), first)
    out = pl.BlockSpec((rows // STEPS, tile), lambda n: (0, n))
    return pl.pallas_call(
        functools.partial(activate_kernel, beams),
        out_shape=(jax.ShapeDtypeStruct((rows // STEPS, columns), BF16),) * STEPS,
        grid=(columns // tile,),
        in_specs=[
            pl.BlockSpec((rows, tile), lambda n: (0, n)),
            full_block(stats.shape),
            pl.BlockSpec((sums.shape[0], tile), lambda n: (0, first // tile + n)),
        ],
        out_specs=(out,) * STEPS,
        compiler_params=pltpu.CompilerParams(vmem_limit_bytes=24 << 20),
    )(total, stats, sums)


def finish_kernel(ranks, width, rank_ref, *refs):
    totals, columns, (sum_ref, out) = refs[:STEPS], refs[STEPS : 2 * STEPS], refs[2 * STEPS :]
    for s in range(STEPS):
        held = columns[s][...].astype(F32)
        lane = lax.broadcasted_iota(jnp.int32, held.shape, 1)

        def column(j, d):
            at = j * 3 * ranks + lax.rem(rank_ref[0] + ranks - d, ranks)
            chosen = (lane == at) | (lane == at + ranks) | (lane == at + 2 * ranks)
            return jnp.sum(jnp.where(chosen, held, 0.0), axis=1, keepdims=True)

        means = [column(0, d) for d in range(ranks)]
        mean = sum(means[1:], means[0]) * (1.0 / ranks)
        square = jnp.zeros_like(mean)
        total = totals[s][...].astype(F32)
        for d in range(ranks):
            away = means[d] - mean
            square = square + column(1, d) + width * away * away
            total = total + away * sum_ref[d : d + 1, :]
        out[s] = (total * lax.rsqrt(square * (1.0 / (width * ranks)) + EPSILON)).astype(BF16)


def finish(totals, sums, width):
    rows = totals[0].shape[0]
    columns = totals[0].shape[1] - LANES
    ranks = lax.axis_size("req")
    rank = lax.axis_index("req").astype(jnp.int32).reshape(1)
    totals = [in_hbm(total) for total in totals]
    return pl.pallas_call(
        functools.partial(finish_kernel, ranks, width),
        out_shape=jax.ShapeDtypeStruct((STEPS, rows, columns), BF16),
        grid=(1,),
        in_specs=[pl.BlockSpec(memory_space=pltpu.SMEM)]
        + [pl.BlockSpec((rows, columns), lambda n: (0, 0))] * STEPS
        + [pl.BlockSpec((rows, LANES), lambda n: (0, columns // LANES))] * STEPS
        + [full_block(sums.shape)],
        out_specs=full_block((STEPS, rows, columns)),
        compiler_params=pltpu.CompilerParams(vmem_limit_bytes=24 << 20),
    )(rank, *totals, *totals, sums)


def update_kernel(ranks, step, place_ref, hidden_ref, down_ref, dense_ref, *refs):
    attended, (mine, other, heads) = refs[: 2 * ranks - 1], refs[2 * ranks - 1 :]
    rows = hidden_ref.shape[0] // ranks
    rank, core = place_ref[0], place_ref[1]

    @pl.when(pl.program_id(0) == 0)
    def _():
        def place(owner, piece):
            at = pl.ds(pl.multiple_of(owner * rows, rows), rows)
            heads[at, :] = piece[step * rows : (step + 1) * rows, :]

        place(rank, attended[0])
        for d in range(1, ranks):
            pl.when(rank >= d)(functools.partial(place, rank - d, attended[d]))
            pl.when(rank + d < ranks)(
                functools.partial(place, rank + d, attended[ranks + d - 1])
            )

    result = jnp.dot(hidden_ref[...], down_ref[...], preferred_element_type=F32) + jnp.dot(
        heads[...], dense_ref[...], preferred_element_type=F32
    )
    half = rows // 2
    for k in range(ranks):
        first = result[k * rows : k * rows + half]
        second = result[k * rows + half : (k + 1) * rows]
        mine[k] = jnp.where(core == 0, first, second).astype(BF16)
        other[k] = jnp.where(core == 0, second, first).astype(BF16)


def layer_update(step, hidden, attended, dense_weight, down_weight):
    ranks = lax.axis_size("req")
    rows, columns = hidden.shape
    head_width, width = dense_weight.shape
    tile = math.gcd(512, width)
    place = jnp.stack([lax.axis_index("req"), lax.axis_index("mlp") % 2]).astype(jnp.int32)
    shape = jax.ShapeDtypeStruct((ranks, rows // ranks // 2, width), BF16)
    out_block = pl.BlockSpec((ranks, rows // ranks // 2, tile), lambda n: (0, 0, n))
    return pl.pallas_call(
        functools.partial(update_kernel, ranks, step),
        out_shape=(shape, shape),
        grid=(width // tile,),
        in_specs=[
            pl.BlockSpec(memory_space=pltpu.SMEM),
            full_block(hidden.shape),
            pl.BlockSpec((columns, tile), lambda n: (0, n)),
            pl.BlockSpec((head_width, tile), lambda n: (0, n)),
        ]
        + [full_block(attended[0].shape)] * (2 * ranks - 1),
        out_specs=(out_block, out_block),
        scratch_shapes=[pltpu.VMEM((rows, head_width), BF16)],
        compiler_params=pltpu.CompilerParams(vmem_limit_bytes=40 << 20),
        cost_estimate=pl.CostEstimate(
            flops=2 * rows * (columns + head_width) * width,
            bytes_accessed=2 * (columns + head_width) * (width + rows),
            transcendentals=0,
        ),
    )(place, in_hbm(hidden), in_hbm(down_weight), in_hbm(dense_weight), *attended)


def rotary_tables(positions):
    lane = jnp.arange(HD, dtype=jnp.int32)[None, :]
    half = ROT // 2
    freq = jnp.exp((lane % half).astype(F32) * (-2.0 * math.log(10000.0) / ROT))
    angles = positions.astype(F32)[:, None] * freq
    cosine = jnp.where(lane < ROT, jnp.cos(angles), 1.0)
    sine = jnp.sin(angles)
    upper = jnp.where(lane < half, -sine, 0.0)
    lower = jnp.where((lane >= half) & (lane < ROT), sine, 0.0)
    return cosine, upper, lower


def in_hbm(array):
    return pltpu.with_memory_space_constraint(array, pltpu.HBM)


def full_block(shape):
    return pl.BlockSpec(shape, lambda *_: (0,) * len(shape))


def turn(value, tables):
    return (
        value * tables[0][...]
        + pltpu.roll(value, HD - ROT // 2, 1) * tables[1][...]
        + pltpu.roll(value, ROT // 2, 1) * tables[2][...]
    )


def store_head(out, value, head, heads, parts, requests):
    rows = requests * BEAM
    for part in range(parts):
        for request in range(requests):
            first = part * STEPS * rows + request * BEAM
            pair = [value[first + s * rows : first + s * rows + BEAM] for s in range(STEPS)]
            at = ((part * requests + request) * heads + head) * STEPS * BEAM
            out[at : at + STEPS * BEAM, :] = jnp.concatenate(pair, axis=0).astype(BF16)


def query_kernel(heads, parts, requests, rank_ref, own_ref, *refs):
    received, (stat_ref, sum_ref, *tables, out) = refs[:-6], refs[-6:]
    for head in range(heads):
        at = slice(head * HD, (head + 1) * HD)
        value = own_ref[0, :, at].astype(F32)
        for piece in received:
            value = value + piece[:, at].astype(F32)
        first = head * 3 * HD
        value = corrected(value, stat_ref, sum_ref[:, first : first + HD])
        store_head(out, turn(value, tables), head, heads, parts, requests)


def split_queries(partial, received, stats, sums, tables, heads, parts, requests):
    rank = lax.axis_index("req").astype(jnp.int32).reshape(1)
    operands = (*received, stats, sums, *tables)
    rows = parts * requests * heads * STEPS * BEAM
    return pl.pallas_call(
        functools.partial(query_kernel, heads, parts, requests),
        out_shape=jax.ShapeDtypeStruct((rows, HD), BF16),
        grid_spec=pltpu.PrefetchScalarGridSpec(
            num_scalar_prefetch=1,
            grid=(1,),
            in_specs=[pl.BlockSpec((1,) + partial.shape[1:], lambda n, r: (r[0], 0, 0))]
            + [full_block(operand.shape) for operand in operands],
            out_specs=full_block((rows, HD)),
        ),
        compiler_params=pltpu.CompilerParams(vmem_limit_bytes=24 << 20),
    )(rank, partial, *operands)


def key_value_kernel(heads, parts, requests, x_ref, stat_ref, sum_ref, *refs):
    tables, outs = refs[:3], refs[3:]
    for head in range(heads):
        for kind, out in enumerate(outs):
            column = (head * 2 + kind) * HD
            value = x_ref[:, column : column + HD].astype(F32)
            column = (head * 3 + kind + 1) * HD
            value = corrected(value, stat_ref, sum_ref[:, column : column + HD])
            if kind == 0:
                value = turn(value, tables)
            store_head(out, value, head, heads, parts, requests)


def split_keys_values(total, stats, sums, tables, heads, parts, requests):
    shape = jax.ShapeDtypeStruct((parts * requests * heads * STEPS * BEAM, HD), BF16)
    return pl.pallas_call(
        functools.partial(key_value_kernel, heads, parts, requests),
        out_shape=(shape, shape),
        compiler_params=pltpu.CompilerParams(vmem_limit_bytes=24 << 20),
    )(total, stats, sums, *tables)


def page_kernel(heads, ranks, own_rows, slot_ref, length_ref, me_ref, k_ref, v_ref, *rest):
    queries, outs = rest[:ranks], rest[ranks : 2 * ranks]
    q_ref, top_ref, sum_ref, out_ref = rest[2 * ranks :]
    step = pl.program_id(0)
    height = heads * STEPS * BEAM
    chunk = STEPS * BEAM
    scale = 1.0 / math.sqrt(HD)

    @pl.when(step == 0)
    def _():
        for d in range(ranks):
            rank = lax.rem(me_ref[0] + ranks - d, ranks)
            q_ref[pl.ds(pl.multiple_of(rank * own_rows, own_rows), own_rows), :] = queries[d][...]
        top_ref[...] = jnp.full(top_ref.shape, NEG_FILL, F32)
        sum_ref[...] = jnp.zeros(sum_ref.shape, F32)
        out_ref[...] = jnp.zeros(out_ref.shape, F32)

    lane = lax.broadcasted_iota(jnp.int32, (height, PAGE), 1)
    found = []
    for g in range(GROUP):
        slot = step * GROUP + g
        owner = slot_ref[0, slot]
        valid = jnp.maximum(owner, 0)
        limit = jnp.where(owner >= 0, length_ref[valid] - slot_ref[1, slot] * PAGE, 0)
        base = pl.multiple_of(valid * height, height)
        scores = []
        for h in range(heads):
            query = q_ref[pl.ds(pl.multiple_of(base + h * chunk, chunk), chunk), :]
            key = k_ref[g, :, h * HD : (h + 1) * HD]
            scores.append(
                lax.dot_general(query, key, (((1,), (1,)), ((), ())), preferred_element_type=F32)
            )
        live = lane < limit
        score = jnp.where(live, jnp.concatenate(scores, axis=0) * scale, NEG_FILL)
        top = jnp.max(score, axis=1, keepdims=True)
        weight = jnp.where(live, jnp.exp(score - top), 0.0)
        total = jnp.sum(weight, axis=1, keepdims=True)
        weight = weight.astype(BF16)
        value = [
            jnp.dot(
                weight[h * chunk : (h + 1) * chunk],
                v_ref[g, :, h * HD : (h + 1) * HD],
                preferred_element_type=F32,
            )
            for h in range(heads)
        ]
        found.append((base, top, total, jnp.concatenate(value, axis=0)))
    for base, top, total, value in found:
        at = pl.ds(base, height)
        old = top_ref[at, :]
        new = jnp.maximum(old, top)
        left = jnp.exp(old - new)
        right = jnp.exp(top - new)
        top_ref[at, :] = new
        sum_ref[at, :] = sum_ref[at, :] * left + total * right
        out_ref[at, :] = out_ref[at, :] * left + value * right

    @pl.when(step == pl.num_programs(0) - 1)
    def _():
        eye = lax.broadcasted_iota(jnp.int32, (LANES, LANES), 0) == lax.broadcasted_iota(
            jnp.int32, (LANES, LANES), 1
        )
        blocks = own_rows // LANES
        for d in range(ranks):
            rank = lax.rem(me_ref[0] + d, ranks)
            levels = []
            for block in range(blocks):
                first = pl.multiple_of(rank * own_rows + block * LANES, LANES)
                total = sum_ref[pl.ds(first, LANES), :]
                some = total > 0.0
                total = jnp.where(some, total, 1.0)
                outs[d][block * LANES : (block + 1) * LANES, :] = (
                    out_ref[pl.ds(first, LANES), :] / total
                ).astype(BF16)
                level = jnp.where(some, top_ref[pl.ds(first, LANES), :] + jnp.log(total), NEG_FILL)
                levels.append(jnp.sum(jnp.where(eye, level, 0.0), axis=0, keepdims=True))
            levels.append(jnp.zeros((STAT_ROWS - blocks, LANES), F32))
            level = jnp.concatenate(levels, axis=0)
            for k in range(3):
                rounded = level.astype(BF16)
                level = level - rounded.astype(F32)
                outs[d][own_rows + k * STAT_ROWS : own_rows + (k + 1) * STAT_ROWS, :] = rounded


def page_attention(queries, keys, values, slot_table, lengths, heads, ranks):
    slots = keys.shape[0]
    own_rows = queries[0].shape[0]
    rows = own_rows * ranks
    me = lax.axis_index("req").astype(jnp.int32).reshape(1)
    out_rows = own_rows + 3 * STAT_ROWS
    shape = jax.ShapeDtypeStruct((out_rows, LANES), BF16)
    page_block = pl.BlockSpec((GROUP, PAGE, heads * HD), lambda g, *_: (g, 0, 0))
    return pl.pallas_call(
        functools.partial(page_kernel, heads, ranks, own_rows),
        out_shape=(shape,) * ranks,
        grid_spec=pltpu.PrefetchScalarGridSpec(
            num_scalar_prefetch=3,
            grid=(slots // GROUP,),
            in_specs=[page_block, page_block] + [full_block((own_rows, HD))] * ranks,
            out_specs=[full_block((out_rows, LANES))] * ranks,
            scratch_shapes=[pltpu.VMEM((rows, HD), BF16)] + [pltpu.VMEM((rows, LANES), F32)] * 3,
        ),
        compiler_params=pltpu.CompilerParams(vmem_limit_bytes=40 << 20),
        cost_estimate=pl.CostEstimate(
            flops=4 * slots * PAGE * heads * HD * STEPS * BEAM,
            bytes_accessed=8 * slots * PAGE * heads * HD * 2,
            transcendentals=slots * PAGE * heads * STEPS * BEAM,
        ),
    )(slot_table, lengths, me, in_hbm(keys), in_hbm(values), *queries)


def merge_kernel(heads, ranks, parts, requests, q_ref, k_ref, v_ref, parent_ref, *rest):
    pieces, out, work = rest[:ranks], rest[ranks], rest[ranks + 1]
    chunk = STEPS * BEAM
    height = heads * chunk
    own_rows = q_ref.shape[0]
    scale = 1.0 / math.sqrt(HD)
    eye = lax.broadcasted_iota(jnp.int32, (LANES, LANES), 0) == lax.broadcasted_iota(
        jnp.int32, (LANES, LANES), 1
    )
    late = lax.broadcasted_iota(jnp.int32, (LANES, 1), 0) % chunk >= BEAM
    levels = []
    for piece in pieces:
        level = jnp.zeros((STAT_ROWS, LANES), F32)
        for k in range(3):
            first = own_rows + k * STAT_ROWS
            level = level + piece[first : first + STAT_ROWS, :].astype(F32)
        levels.append(level)
    for block in range(own_rows // LANES):
        at = slice(block * LANES, (block + 1) * LANES)
        query = q_ref[at, :].astype(F32)
        key = k_ref[at, :].astype(F32)
        value = v_ref[at, :].astype(F32)
        held_keys, held_values = [], []
        for tile in range(LANES // chunk):
            first = tile * chunk
            request = (block * LANES + first) // height
            parent = parent_ref[request * BEAM : (request + 1) * BEAM, :]
            for held, source in ((held_keys, key), (held_values, value)):
                chosen = jnp.zeros((BEAM, HD), F32)
                for beam in range(BEAM):
                    row = source[first + beam : first + beam + 1, :]
                    chosen = jnp.where(parent == beam, row, chosen)
                held += [jnp.zeros((BEAM, HD), F32), chosen]
        held_key = jnp.concatenate(held_keys, axis=0)
        held_value = jnp.concatenate(held_values, axis=0)
        own = jnp.sum(query * key, axis=1, keepdims=True) * scale
        past = jnp.sum(query * held_key, axis=1, keepdims=True) * scale
        past = jnp.where(late, past, NEG_FILL)
        columns = [
            jnp.sum(jnp.where(eye, level[block : block + 1, :], 0.0), axis=1, keepdims=True)
            for level in levels
        ]
        top = functools.reduce(jnp.maximum, columns, jnp.maximum(own, past))
        own = jnp.exp(own - top)
        past = jnp.where(late, jnp.exp(past - top), 0.0)
        total = own + past
        result = own * value + past * held_value
        for column, piece in zip(columns, pieces):
            factor = jnp.exp(column - top)
            total = total + factor
            result = result + factor * piece[at, :].astype(F32)
        work[at, :] = result / total
    rows = requests * BEAM
    for part in range(parts):
        for request in range(0, requests, 2):
            for head in range(heads):
                for s in range(STEPS):
                    tiles = []
                    for r in (request, request + 1):
                        first = (part * requests + r) * height + head * chunk + s * BEAM
                        tiles.append(work[first : first + BEAM, :])
                    first = (s * parts + part) * rows + request * BEAM
                    out[first : first + 2 * BEAM, head * HD : (head + 1) * HD] = jnp.concatenate(
                        tiles, axis=0
                    ).astype(BF16)


def merge(queries, keys, values, parents, pieces, heads, parts, requests):
    ranks = len(pieces)
    rows = STEPS * parts * requests * BEAM
    return pl.pallas_call(
        functools.partial(merge_kernel, heads, ranks, parts, requests),
        out_shape=jax.ShapeDtypeStruct((rows, heads * HD), BF16),
        scratch_shapes=[pltpu.VMEM(queries.shape, F32)],
        compiler_params=pltpu.CompilerParams(vmem_limit_bytes=32 << 20),
    )(queries, keys, values, parents, *pieces)


def shards(
    inputs,
    norm_gains,
    attn_weight,
    up_weight,
    dense_weight,
    down_weight,
    next_weight,
    cache_keys,
    cache_values,
    lengths,
    slot_table,
    parents,
):
    ranks = lax.axis_size("req")
    own_count = parents.shape[1]
    beams = inputs.shape[1]
    width = inputs.shape[2]
    parts = own_count // beams
    requests = beams // BEAM
    own_requests = own_count // BEAM
    heads = dense_weight.shape[0] // HD
    rank = lax.axis_index("req")
    assert parts == 2 and lax.axis_size("mlp") == 2 * ranks

    own_lengths = lax.dynamic_slice_in_dim(lengths, rank * own_requests, own_requests, 0)
    positions = jnp.broadcast_to(
        own_lengths.reshape(parts, 1, requests, 1)
        + jnp.arange(STEPS, dtype=jnp.int32).reshape(1, STEPS, 1, 1),
        (parts, STEPS, requests, BEAM),
    ).reshape(-1)
    tables = rotary_tables(positions)
    parent_wide = jnp.broadcast_to(parents[0][:, None], (own_count, LANES))

    with jax.named_scope("inputs_gather"):
        pieces = gather_pieces(inputs.reshape(STEPS * beams, width))
    with jax.named_scope("qkv"):
        query, key_value, stats, mlp_in = project(
            pieces, norm_gains[:2], attn_weight, (HD, 2 * HD)
        )
        key_value = lax.psum_scatter(key_value, "req", scatter_dimension=0, tiled=True)
        query = query.reshape(ranks, -1, query.shape[1])
        received = [
            rotated(
                lax.dynamic_index_in_dim(query, (rank + d) % ranks, 0, keepdims=False), "req", d
            )
            for d in range(1, ranks)
        ]
    with jax.named_scope("weight_sums"):
        weights = (attn_weight, up_weight, next_weight)
        sums = [weight_sums(norm_gains[k], w) for k, w in enumerate(weights)]
        sums = jnp.concatenate(exchange(jnp.concatenate(sums, axis=1)))
        up_first = attn_weight.shape[1]
        next_first = up_first + up_weight.shape[1]
    with jax.named_scope("statistics"):
        stats = stat_columns(*own_statistics(stats, width, STEPS * beams))
    with jax.named_scope("queries"):
        queries = split_queries(query, received, stats, sums, tables, heads, parts, requests)
        queries_all = exchange(queries)
    with jax.named_scope("up"):
        up = jnp.dot(after(mlp_in, queries), up_weight, preferred_element_type=F32).astype(BF16)
        up = lax.psum_scatter(up, "req", scatter_dimension=0, tiled=True)
    with jax.named_scope("pages"):
        pieces = page_attention(
            queries_all, cache_keys, cache_values, slot_table, lengths, heads, ranks
        )
        pieces = [pieces[0]] + [rotated(pieces[d], "req", d) for d in range(1, ranks)]
    with jax.named_scope("merge"):
        key_value = after(key_value, pieces[0])
        keys, values = split_keys_values(
            key_value, stats, sums, tables, heads, parts, requests
        )
        attended = merge(queries, keys, values, parent_wide, pieces, heads, parts, requests)
        rights, lefts = line_gather(attended)
        attended_all = [attended, *rights, *lefts]
    with jax.named_scope("activated"):
        activated = activate(after(up, attended), stats, sums, up_first, beams)
        activated = [lax.all_gather(own, "req", axis=0, tiled=True) for own in activated]
    layers, totals = [], []
    for s in range(STEPS):
        with jax.named_scope(f"down_{s}"):
            mine, other = layer_update(s, activated[s], attended_all, dense_weight, down_weight)
            layer = (inputs[s].astype(F32) + scatter_sum(mine, other)).astype(BF16)
            layers.append(layer)
        with jax.named_scope(f"next_{s}"):
            partial = project_next(gather_pieces(layer), norm_gains[2:], next_weight)
            if s + 1 < STEPS:
                activated[s + 1] = after(activated[s + 1], partial)
            totals.append(lax.psum_scatter(partial, "req", scatter_dimension=0, tiled=True))
    return jnp.stack(layers), finish(totals, sums[:, next_first:], width)


def solution(mesh):
    in_specs = (
        P(None, "mlp", "req"),
        P(None, "req"),
        P("req", "mlp"),
        P("req", "mlp"),
        P("mlp", "req"),
        P("mlp", "req"),
        P("req", "mlp"),
        P("req", None, "mlp"),
        P("req", None, "mlp"),
        P(),
        P(None, "req"),
        P(None, "req"),
    )
    out_specs = (P(None, "mlp", "req"), P(None, "req", "mlp"))
    return jax.shard_map(shards, mesh=mesh, in_specs=in_specs, out_specs=out_specs, check_vma=False)
```
